32 devices in a mesh: blk: 8 (over z, x), rep: 4 (over y, core).
Axes of the slice: x: 2, y: 2, z: 4, core: 2. Of those that a mesh axis runs over, the one named last changes fastest.
Arguments:
- hidden: bfloat16 [4, 8, 256, 768], P('rep', 'blk'), may hold values from -6 to 6
- store: bfloat16 [4, 128, 768], P('rep', 'blk'), may hold values from -6 to 6
- retrieved: int32 [4, 8, 256, 64], P('rep', 'blk'), may hold values from 0 to 127, as said below
- live: int32 [4, 8, 256, 64], P('rep', 'blk'), may hold values 0 or 1
- lengths: int32 [4, 8], P('rep', 'blk'), may hold values from 64 to 256, as said below
- self_qkv: bfloat16 [768, 2304], replicated, may hold values from -0.21875 to 0.21875
- self_bias: float32 [2, 768], replicated, may hold values from -0.6 to 0.6
- self_out: bfloat16 [768, 768], replicated, may hold values from -1.75 to 1.75
- self_out_bias: float32 [768], replicated, may hold values from -0.6 to 0.6
- norm1: float32 [2, 768], replicated, may hold values from -0.3 to 1.3, as said below
- cross_q: bfloat16 [768, 768], replicated, may hold values from -0.21875 to 0.21875
- cross_q_bias: float32 [768], replicated, may hold values from -0.6 to 0.6
- cross_kv: bfloat16 [768, 1536], replicated, may hold values from -0.21875 to 0.21875
- cross_v_bias: float32 [768], replicated, may hold values from -0.6 to 0.6
- cross_out: bfloat16 [768, 768], replicated, may hold values from -1.75 to 1.75
- cross_out_bias: float32 [768], replicated, may hold values from -0.6 to 0.6
- norm2: float32 [2, 768], replicated, may hold values from -0.3 to 1.3, as said below
- ffn_in: bfloat16 [768, 3072], replicated, may hold values from -0.21875 to 0.21875
- ffn_in_bias: float32 [3072], replicated, may hold values from -0.6 to 0.6
- ffn_out: bfloat16 [3072, 768], replicated, may hold values from -0.109375 to 0.109375
- ffn_out_bias: float32 [768], replicated, may hold values from -0.6 to 0.6
- norm3: float32 [2, 768], replicated, may hold values from -0.3 to 1.3, as said below
- cotangent: bfloat16 [4, 8, 256, 768], P('rep', 'blk'), may hold values from -6 to 6
Outputs:
- output: bfloat16 [4, 8, 256, 768], P('rep', 'blk')
- d_hidden: float32 [4, 8, 256, 768], P('rep', 'blk')
- d_store: float32 [4, 128, 768], P('rep', 'blk')
- d_self_qkv: float32 [768, 2304], P('blk')
- d_self_bias: float32 [2, 768], P(None, 'blk')
- d_self_out: float32 [768, 768], P('blk')
- d_self_out_bias: float32 [768], P('blk')
- d_norm1: float32 [2, 768], P(None, 'blk')
- d_cross_q: float32 [768, 768], P('blk')
- d_cross_q_bias: float32 [768], P('blk')
- d_cross_kv: float32 [768, 1536], P('blk')
- d_cross_v_bias: float32 [768], P('blk')
- d_cross_out: float32 [768, 768], P('blk')
- d_cross_out_bias: float32 [768], P('blk')
- d_norm2: float32 [2, 768], P(None, 'blk')
- d_ffn_in: float32 [768, 3072], P('blk')
- d_ffn_in_bias: float32 [3072], P('blk')
- d_ffn_out: float32 [3072, 768], P('blk')
- d_ffn_out_bias: float32 [768], P('blk')
- d_norm3: float32 [2, 768], P(None, 'blk')
The draws below stay inside these ranges and needn't reach their ends.
Inputs may be any that keep to these rules, and one draw needn't show every extreme that they name: `retrieved`: each query names 64 different slots: one in each of 64 cyclic runs of 2 consecutive slots that start at a shift of the query's own. `lengths`: in each group one summary has exactly 64 tokens and another exactly 256; rows at or past a summary's length are padding. `norm1`: row 0 is a gain, row 1 a shift. `norm2`: row 0 is a gain, row 1 a shift. `norm3`: row 0 is a gain, row 1 a shift.
All inputs are finite; a program needn't handle non-finite values. No bound on the sum of `live` on one device may be relied on, other than what follows from the above.
Results may differ from the reference program's by a relative error of at most 0.025.
Values may be sent and summed in bfloat16 or wider, within the bound.
A program may use at most 192 MiB of HBM per device.

```python
from functools import partial
import jax
import jax.numpy as jnp
from jax import lax

D = 768
HEADS = 12
HD = 64
FF = 3072
LEN = 256
MIN_LEN = 64
TOPK = 64
SLOTS = 128
GROUPS = 4
SEQ_GROUP = 8


def gain_shift_rows(base_key):
    gain_key, shift_key = jax.random.split(base_key)
    gain_row = 1.0 + 0.3 * jax.random.uniform(gain_key, (D,), jnp.float32, -1.0, 1.0)
    shift_row = 0.3 * jax.random.uniform(shift_key, (D,), jnp.float32, -1.0, 1.0)
    return jnp.stack([gain_row, shift_row])


def draw_norm1(key, part):
    key = jax.random.fold_in(key, 21)
    return gain_shift_rows(key)


def draw_norm2(key, part):
    key = jax.random.fold_in(key, 22)
    return gain_shift_rows(key)


def draw_norm3(key, part):
    key = jax.random.fold_in(key, 23)
    return gain_shift_rows(key)


def draw_retrieved(key, part):
    key = jax.random.fold_in(key, 11)
    offset_key, shift_key = jax.random.split(key)
    run_size = SLOTS // TOPK
    offsets = jax.random.randint(offset_key, (GROUPS, SEQ_GROUP, LEN, TOPK), 0, run_size)
    shifts = jax.random.randint(shift_key, (GROUPS, SEQ_GROUP, LEN, 1), 0, SLOTS)
    starts = jnp.arange(TOPK, dtype=jnp.int32) * run_size
    return ((starts + offsets + shifts) % SLOTS).astype(jnp.int32)


def draw_lengths(key, part):
    key = jax.random.fold_in(key, 13)
    draw_key, long_key, short_key = jax.random.split(key, 3)
    drawn = jax.random.randint(draw_key, (GROUPS, SEQ_GROUP), MIN_LEN, LEN + 1)
    longest = jax.random.randint(long_key, (GROUPS, 1), 0, SEQ_GROUP)
    shortest = (longest + 1 + jax.random.randint(short_key, (GROUPS, 1), 0, SEQ_GROUP - 1)) % SEQ_GROUP
    places = jnp.arange(SEQ_GROUP, dtype=jnp.int32)[None, :]
    drawn = jnp.where(places == longest, LEN, drawn)
    return jnp.where(places == shortest, MIN_LEN, drawn).astype(jnp.int32)


def set_ends(values, own_key, smallest, top_value):
    place = [jax.random.randint(jax.random.fold_in(own_key, axis), (), 0, length) for axis, length in enumerate(values.shape)]
    widest = values.shape.index(max(values.shape))
    next_to = place[:widest] + [(place[widest] + 1) % values.shape[widest]] + place[widest + 1:]
    return values.at[tuple(place)].set(smallest).at[tuple(next_to)].set(top_value)


def spiked(values, rng, source, target, blocks, factor):
    owner, partner = [(jnp.arange(values.shape[dim]) // (values.shape[dim] // blocks)).reshape([-1 if axis == dim else 1 for axis in range(values.ndim)]) for dim in (source, target)]
    chosen = jax.random.permutation(rng, blocks)[partner]
    strong = (owner == chosen) | (owner == (partner + blocks // 2) % blocks)
    return jnp.where(strong, factor * values, values)


def level_of(stream_key, extent, cuts, low, largest):
    loudness = 1.0
    for position, shards_of in cuts:
        steps = jax.random.uniform(jax.random.fold_in(jax.random.fold_in(stream_key, 6), position), (shards_of,), jnp.float32, low / len(cuts), largest / len(cuts))
        loudness = loudness * jnp.repeat(jnp.exp(steps), extent[position] // shards_of).reshape((-1,) + (1,) * (len(extent) - 1 - position))
    return loudness


def scatter_about(key, extent, scale, reach, cuts=(), kind=jnp.bfloat16):
    values = jax.random.normal(key, extent, jnp.float32) * scale
    if len(cuts) > 0:
        values = level_of(key, extent, cuts, -0.22, 0.18) * values
    return jnp.clip(values, min=-reach, max=reach).astype(kind)


def bell_draw_with(key, shape, width, bound, cuts, heavy, held_as=jnp.bfloat16):
    values = width * jax.random.normal(key, shape, jnp.float32)
    if cuts:
        values = values * level_of(key, shape, cuts, -0.22, 0.18)
    return jnp.clip(spiked(values, jax.random.fold_in(key, 3), *heavy), -bound, bound).astype(held_as)


def setup_inputs(seed: int = 0) -> dict:
    keys = jax.random.split(jax.random.key(seed), 24)
    hidden = bell_draw_with(keys[0], (GROUPS, SEQ_GROUP, LEN, D), 1.0, 6.0, ((0, 4), (1, 8)), (1, 3, 8, 2.0))
    store = bell_draw_with(keys[1], (GROUPS, SLOTS, D), 1.0, 6.0, ((0, 4), (1, 8)), (1, 2, 8, 2.0))
    retrieved = draw_retrieved(jax.random.fold_in(keys[23], 71), 0)
    live = set_ends((jax.random.randint(keys[3], (GROUPS, SEQ_GROUP, LEN, TOPK), 0, 8) < 7).astype(jnp.int32), jax.random.fold_in(keys[3], 1), 0, 1)
    lengths = draw_lengths(jax.random.fold_in(keys[23], 71), 0)
    self_qkv = scatter_about(keys[5], (D, 3 * D), D ** -0.5, 0.21875)
    self_bias = scatter_about(keys[6], (2, D), 0.1, 0.6, (), jnp.float32)
    self_out = scatter_about(keys[7], (D, D), (max(D // 64, 8)) ** -0.5, 1.75)
    self_out_bias = scatter_about(keys[8], (D,), 0.1, 0.6, (), jnp.float32)
    norm1 = draw_norm1(jax.random.fold_in(keys[23], 71), 0)
    cross_q = scatter_about(keys[10], (D, D), D ** -0.5, 0.21875)
    cross_q_bias = scatter_about(keys[11], (D,), 0.1, 0.6, (), jnp.float32)
    cross_kv = scatter_about(keys[12], (D, 2 * D), D ** -0.5, 0.21875)
    cross_v_bias = scatter_about(keys[13], (D,), 0.1, 0.6, (), jnp.float32)
    cross_out = scatter_about(keys[14], (D, D), (max(D // 64, 8)) ** -0.5, 1.75)
    cross_out_bias = scatter_about(keys[15], (D,), 0.1, 0.6, (), jnp.float32)
    norm2 = draw_norm2(jax.random.fold_in(keys[23], 71), 0)
    ffn_in = scatter_about(keys[17], (D, FF), D ** -0.5, 0.21875)
    ffn_in_bias = scatter_about(keys[18], (FF,), 0.1, 0.6, (), jnp.float32)
    ffn_out = scatter_about(keys[19], (FF, D), FF ** -0.5, 0.109375)
    ffn_out_bias = scatter_about(keys[20], (D,), 0.1, 0.6, (), jnp.float32)
    norm3 = draw_norm3(jax.random.fold_in(keys[23], 71), 0)
    cotangent = scatter_about(keys[22], (GROUPS, SEQ_GROUP, LEN, D), 1.0, 6.0, ((0, 4), (1, 8)))
    return {"hidden": hidden, "store": store, "retrieved": retrieved, "live": live, "lengths": lengths, "self_qkv": self_qkv, "self_bias": self_bias, "self_out": self_out, "self_out_bias": self_out_bias, "norm1": norm1, "cross_q": cross_q, "cross_q_bias": cross_q_bias, "cross_kv": cross_kv, "cross_v_bias": cross_v_bias, "cross_out": cross_out, "cross_out_bias": cross_out_bias, "norm2": norm2, "ffn_in": ffn_in, "ffn_in_bias": ffn_in_bias, "ffn_out": ffn_out, "ffn_out_bias": ffn_out_bias, "norm3": norm3, "cotangent": cotangent}


@jax.custom_vjp
def low(v):
    return lax.optimization_barrier(v.astype(jnp.bfloat16)).astype(jnp.float32)

@jax.custom_vjp
def low_back(v):
    return v

def low_keep(v):
    return (low(v), None)

def low_pass(kept, grad):
    return (grad,)

def back_keep(v):
    return (v, None)

def back_low(kept, grad):
    return (low(grad),)
low.defvjp(low_keep, low_pass)
low_back.defvjp(back_keep, back_low)
EPS = 1e-05
NEG = -1e+30
HIGH = lax.Precision.HIGHEST

def product(left_op, right_op):
    return jnp.dot(left_op, right_op, precision=HIGH)

def layer_norm(resid_in, norm_params):
    mean_val = lax.optimization_barrier(jnp.mean(resid_in, axis=-1, keepdims=True))
    centered = resid_in - mean_val
    variance = lax.optimization_barrier(jnp.mean(centered * centered, axis=-1, keepdims=True))
    return centered * lax.rsqrt(variance + EPS) * norm_params[0] + norm_params[1]

def attend(queries, key_rows, value_rows, allowed, scaling):
    q_heads = queries.reshape(queries.shape[0], HEADS, HD)
    k_heads = key_rows.reshape(key_rows.shape[0], HEADS, HD)
    v_heads = value_rows.reshape(value_rows.shape[0], HEADS, HD)
    raw_scores = jnp.einsum('qhd,khd->hqk', q_heads, k_heads, precision=HIGH)
    scores = jnp.where(allowed[None], low_back(raw_scores * scaling), NEG)
    weights = jax.nn.softmax(scores, axis=-1)
    mixed = jnp.einsum('hqk,khd->qhd', low(weights), v_heads, precision=HIGH)
    return mixed.reshape(queries.shape[0], HEADS * HD)

def sequence(params, store_keys, store_values, tokens, store_mask, length):
    self_qkv, self_bias, self_out, self_out_bias, norm1, cross_q, cross_q_bias, cross_out, cross_out_bias, norm2, ffn_in, ffn_in_bias, ffn_out, ffn_out_bias, norm3 = params
    scaling = HD ** (-0.5)
    projected = product(tokens, self_qkv)
    queries = low(low_back(projected[:, :D] + self_bias[0]))
    key_rows = low(low_back(projected[:, D:2 * D]))
    value_rows = low(low_back(projected[:, 2 * D:] + self_bias[1]))
    places = jnp.arange(LEN, dtype=jnp.int32)
    allowed = (places[None, :] <= places[:, None]) & (places[None, :] < length)
    self_mix = low(low_back(attend(queries, key_rows, value_rows, allowed, scaling)))
    first_res = tokens + low_back(product(self_mix, self_out) + self_out_bias)
    first = layer_norm(first_res, norm1)
    cross_query = low(low_back(product(low(first), cross_q) + cross_q_bias))
    cross_mix = low(low_back(attend(cross_query, store_keys, store_values, store_mask, scaling)))
    second_res = first + low_back(product(cross_mix, cross_out) + cross_out_bias)
    second = layer_norm(second_res, norm2)
    inner = low_back(product(low(second), ffn_in) + ffn_in_bias)
    activated = low(jax.nn.gelu(inner, approximate=False))
    third_res = second + low_back(product(activated, ffn_out) + ffn_out_bias)
    return layer_norm(third_res, norm3)

def group_forward(masks, group_lengths, tokens_all, states, self_qkv, self_bias, self_out, self_out_bias, norm1, cross_q, cross_q_bias, cross_kv, cross_v_bias, cross_out, cross_out_bias, norm2, ffn_in, ffn_in_bias, ffn_out, ffn_out_bias, norm3):
    projected = product(states, cross_kv)
    store_keys = low(projected[:, :D])
    store_values = low(projected[:, D:] + cross_v_bias)
    params = (self_qkv, self_bias, self_out, self_out_bias, norm1, cross_q, cross_q_bias, cross_out, cross_out_bias, norm2, ffn_in, ffn_in_bias, ffn_out, ffn_out_bias, norm3)

    def one_summary(item):
        tokens, store_mask, length = item
        return sequence(params, store_keys, store_values, tokens, store_mask, length)
    return lax.map(jax.checkpoint(one_summary), (tokens_all, masks, group_lengths))

def store_masks(chosen, live_group):
    number = chosen.shape[0] * chosen.shape[1]
    flat_chosen = chosen.reshape(number, TOPK).astype(jnp.int32)
    usable = (live_group.reshape(number, TOPK) > 0) | (jnp.arange(TOPK, dtype=jnp.int32) == 0)[None, :]
    row_ids = jnp.arange(number, dtype=jnp.int32)[:, None]
    table_mask = jnp.zeros((number, SLOTS), jnp.bool_).at[row_ids, flat_chosen].set(usable)
    return table_mask.reshape(chosen.shape[0], LEN, SLOTS)

def reference(hidden, store, retrieved, live, lengths, self_qkv, self_bias, self_out, self_out_bias, norm1, cross_q, cross_q_bias, cross_kv, cross_v_bias, cross_out, cross_out_bias, norm2, ffn_in, ffn_in_bias, ffn_out, ffn_out_bias, norm3, cotangent):
    weights_all = tuple((weight.astype(jnp.float32) for weight in (self_qkv, self_bias, self_out, self_out_bias, norm1, cross_q, cross_q_bias, cross_kv, cross_v_bias, cross_out, cross_out_bias, norm2, ffn_in, ffn_in_bias, ffn_out, ffn_out_bias, norm3)))
    outputs = []
    d_hiddens = []
    d_stores = []
    totals = None
    places = jnp.arange(LEN, dtype=jnp.int32)
    for group_index in range(GROUPS):
        masks = store_masks(retrieved[group_index], live[group_index])
        runner = partial(group_forward, masks, lengths[group_index])
        result, pull = jax.vjp(runner, hidden[group_index].astype(jnp.float32), store[group_index].astype(jnp.float32), *weights_all)
        row_live = (places[None, :] < lengths[group_index][:, None]).astype(jnp.float32)
        grads = pull(cotangent[group_index].astype(jnp.float32) * row_live[:, :, None])
        outputs.append(result.astype(jnp.bfloat16))
        d_hiddens.append(grads[0])
        d_stores.append(grads[1])
        if totals is None:
            totals = tuple(grads[2:])
        else:
            totals = tuple((acc_grad + new_grad for acc_grad, new_grad in zip(totals, grads[2:])))
    return (jnp.stack(outputs), jnp.stack(d_hiddens), jnp.stack(d_stores), totals[0], totals[1], totals[2], totals[3], totals[4], totals[5], totals[6], totals[7], totals[8], totals[9], totals[10], totals[11], totals[12], totals[13], totals[14], totals[15], totals[16])
```

```python
import functools

import jax
import jax.numpy as jnp
from jax import lax
from jax.experimental import pallas as pl
from jax.experimental.pallas import tpu as pltpu
from jax.sharding import PartitionSpec as P

D = 768
HEADS = 12
HD = 64
FF = 3072
EPS = 1e-05
NEG = -1e30
BF = jnp.bfloat16
F32 = jnp.float32
MESH = pl.DeviceIdType.MESH
VMEM_LIMIT = 62 * 2**20

C_INNER, C_PROJ, C_SB, C_CQ, C_CB, C_FB, C_ALL = 0, 3072, 5376, 6144, 6912, 7680, 8448
R_SECOND, R_TOK, R_SMIX, R_FIRST, R_CMIX, R_ALL = 0, 768, 1536, 2304, 3072, 3840
N_VEC = 17


def dot(a, b):
    return lax.dot_general(a, b, (((1,), (0,)), ((), ())), preferred_element_type=F32)


def dot_nt(a, b):
    return lax.dot_general(a, b, (((1,), (1,)), ((), ())), preferred_element_type=F32)


def dot_tn(a, b):
    return lax.dot_general(a, b, (((0,), (0,)), ((), ())), preferred_element_type=F32)


def at(index, size):
    return pl.ds(pl.multiple_of(index * size, size), size)


def half_mask(half):
    lane = lax.broadcasted_iota(jnp.int32, (1, 2 * HD), 1)
    return ((lane >= HD) if half else (lane < HD)).astype(F32).astype(BF)


def partial_rows(values):
    rows, width = values.shape
    return jnp.sum(values.reshape(rows // 8, 8, width), axis=0)


def total_row(values):
    return jnp.sum(values, axis=0, keepdims=True)


def gelu_and_slope(v):
    cdf = 0.5 * (1.0 + lax.erf(v * 0.7071067811865476))
    return v * cdf, cdf + v * (jnp.exp(-0.5 * v * v) * 0.3989422804014327)


def norm_rows(r):
    centered = r - jnp.mean(r, axis=-1, keepdims=True)
    rstd = lax.rsqrt(jnp.mean(centered * centered, axis=-1, keepdims=True) + EPS)
    return centered * rstd, rstd


def norm_rows_back(grad, xhat, rstd, gain):
    e = grad * gain
    mean_e = jnp.mean(e, axis=-1, keepdims=True)
    mean_x = jnp.mean(e * xhat, axis=-1, keepdims=True)
    return (e - mean_e - xhat * mean_x) * rstd


def row_blocks(rows, block, body, init):
    return lax.fori_loop(0, rows // block, lambda i, c: body(at(i, block), i, c), init)


def attend(q_ref, k_ref, vt_ref, bias_ref, p_ref, mix_t_ref):
    def pair(j, _):
        cols = at(j, 2 * HD)
        q2, k2 = q_ref[:, cols], k_ref[:, cols]
        for half in range(2):
            h = 2 * j + half
            st = dot_nt(k2 * half_mask(half), q2) + bias_ref[...]
            e = jnp.exp(st - jnp.max(st, axis=0, keepdims=True))
            p = (e * (1.0 / jnp.sum(e, axis=0, keepdims=True))).astype(BF)
            p_ref[h] = p
            rows = at(h, HD)
            mix_t_ref[rows, :] = dot(vt_ref[rows, :], p).astype(BF)
        return 0

    lax.fori_loop(0, HEADS // 2, pair, 0)


def attend_back(p_ref, dmix_ref, q_ref, v_ref, kt_ref, dq_t_ref, put):
    def pair(j, _):
        cols = at(j, 2 * HD)
        dm2, q2, v2 = dmix_ref[:, cols], q_ref[:, cols], v_ref[:, cols]
        dk = dv = None
        for half in range(2):
            h = 2 * j + half
            mask = half_mask(half)
            dp = dot_nt(v2 * mask, dm2)
            pb = p_ref[h]
            p = pb.astype(F32)
            t = p * dp
            ds = (t - p * jnp.sum(t, axis=0, keepdims=True)).astype(BF)
            rows = at(h, HD)
            dq_t_ref[rows, :] = dot(kt_ref[rows, :], ds).astype(BF)
            dk_h, dv_h = dot(ds, q2 * mask), dot(pb, dm2 * mask)
            dk = dk_h if dk is None else dk + dk_h
            dv = dv_h if dv is None else dv + dv_h
        put(j, dk, dv)
        return 0

    lax.fori_loop(0, HEADS // 2, pair, 0)


def layer_kernel(
    tokens, states, retrieved, live, lengths, self_bias, self_out_bias, norm1, cq_bias, cv_bias, co_bias, norm2,
    fi_bias, fo_bias, norm3, cotangent, w_qkv_h, w_so_h, w_cq_h, w_ckv_h, w_co_h, w_fi_h, w_fo_h,
    result, d_hidden, xt, act_t, dmat, dkv, dstore, vec,
    w_qkv, w_so, w_cq, w_ckv, w_co, w_fi, w_fo, w_sem,
    q, k, v, vt, bias_s, p_s, sk, sv, svt, bias_c, p_c, cquery, mix_b, dmix,
    acc, acc2, first, xhat1, xhat2, second, sec_b, act, slope, d_res, dqt, rstd1, rstd2,
):
    rows = tokens.shape[0]
    slots = states.shape[0]
    length = lengths[0, 0]
    scale = HD**-0.5
    copies = []
    for i, (src, dst) in enumerate(
        [(w_qkv_h, w_qkv), (w_so_h, w_so), (w_cq_h, w_cq), (w_ckv_h, w_ckv), (w_co_h, w_co), (w_fi_h, w_fi), (w_fo_h, w_fo)]
    ):
        copies.append(pltpu.make_async_copy(src, dst, w_sem.at[i]))
        copies[-1].start()

    key_at = lax.broadcasted_iota(jnp.int32, (rows, rows), 0)
    query_at = lax.broadcasted_iota(jnp.int32, (rows, rows), 1)
    bias_s[...] = jnp.where((key_at <= query_at) & (key_at < length), 0.0, NEG)
    topk = retrieved.shape[1]
    slot_rank = lax.broadcasted_iota(jnp.int32, (rows, topk), 1)
    chosen = jnp.where((live[...] > 0) | (slot_rank == 0), retrieved[...], -1).T

    def mask_rows(i, _):
        ids = lax.broadcasted_iota(jnp.int32, (32, rows), 0) + i * 32
        hit = jnp.zeros((32, rows), jnp.bool_)
        for j in range(topk):
            hit = hit | (ids == chosen[j : j + 1, :])
        bias_c[at(i, 32), :] = jnp.where(hit, 0.0, NEG)
        return 0

    lax.fori_loop(0, slots // 32, mask_rows, 0)

    xt[R_TOK : R_TOK + D, :] = tokens[...].T
    copies[0].wait()
    q[...] = (dot(tokens[...], w_qkv[:, :D]) + self_bias[0:1, :]).astype(BF) * scale
    k[...] = dot(tokens[...], w_qkv[:, D : 2 * D]).astype(BF)
    v[...] = (dot(tokens[...], w_qkv[:, 2 * D :]) + self_bias[1:2, :]).astype(BF)
    vt[...] = v[...].T
    attend(q, k, vt, bias_s, p_s, xt.at[R_SMIX : R_SMIX + D])
    vt[...] = k[...].T * scale
    copies[1].wait()
    mix_b[...] = xt[R_SMIX : R_SMIX + D, :].T
    acc[...] = dot(mix_b[...], w_so[...])

    def ln1(rs, i, c):
        xhat, rstd = norm_rows(tokens[rs, :].astype(F32) + acc[rs, :] + self_out_bias[...][None, :])
        f = xhat * norm1[0:1, :] + norm1[1:2, :]
        xhat1[rs, :] = xhat
        rstd1[rs, :] = rstd
        first[rs, :] = f
        sec_b[rs, :] = f.astype(BF)
        return c

    row_blocks(rows, 32, ln1, 0)
    xt[R_FIRST : R_FIRST + D, :] = sec_b[...].T

    copies[2].wait()
    cquery[...] = (dot(sec_b[...], w_cq[...]) + cq_bias[...][None, :]).astype(BF) * scale
    copies[3].wait()
    sk[...] = dot(states[...], w_ckv[:, :D]).astype(BF)
    sv[...] = (dot(states[...], w_ckv[:, D:]) + cv_bias[...][None, :]).astype(BF)
    svt[...] = sv[...].T
    attend(cquery, sk, svt, bias_c, p_c, xt.at[R_CMIX : R_CMIX + D])
    svt[...] = sk[...].T * scale
    copies[4].wait()
    mix_b[...] = xt[R_CMIX : R_CMIX + D, :].T
    acc[...] = dot(mix_b[...], w_co[...])

    def ln2(rs, i, c):
        xhat, rstd = norm_rows(first[rs, :] + acc[rs, :] + co_bias[...][None, :])
        s = xhat * norm2[0:1, :] + norm2[1:2, :]
        xhat2[rs, :] = xhat
        rstd2[rs, :] = rstd
        second[rs, :] = s
        sec_b[rs, :] = s.astype(BF)
        return c

    row_blocks(rows, 32, ln2, 0)
    xt[R_SECOND : R_SECOND + D, :] = sec_b[...].T

    copies[5].wait()
    copies[6].wait()
    acc[...] = jnp.zeros_like(acc)

    def ffn(j, _):
        cols = at(j, D)
        acc2[...] = dot(sec_b[...], w_fi[:, cols])
        bias = fi_bias[pl.ds(j, 1), :]

        def gelu(rs, i, c):
            a, s = gelu_and_slope(acc2[rs, :] + bias)
            act[rs, :] = a.astype(BF)
            slope[rs, cols] = s.astype(BF)
            return c

        row_blocks(rows, 16, gelu, 0)
        act_t[cols, :] = act[...].T
        acc[...] += dot(act[...], w_fo[cols, :])
        return 0

    lax.fori_loop(0, FF // D, ffn, 0)
    zero = jnp.zeros((8, D), F32)

    def ln3(rs, i, c):
        xhat, rstd = norm_rows(second[rs, :] + acc[rs, :] + fo_bias[...][None, :])
        result[rs, :] = (xhat * norm3[0:1, :] + norm3[1:2, :]).astype(BF)
        place = lax.broadcasted_iota(jnp.int32, (32, 1), 0) + i * 32
        g = cotangent[rs, :].astype(F32) * jnp.where(place < length, 1.0, 0.0)
        d = norm_rows_back(g, xhat, rstd, norm3[0:1, :])
        d_res[rs, :] = d
        db = d.astype(BF)
        dmat[rs, C_FB : C_FB + D] = db
        return (c[0] + partial_rows(g * xhat), c[1] + partial_rows(g), c[2] + partial_rows(db.astype(F32)))

    sums = row_blocks(rows, 32, ln3, (zero, zero, zero))
    vec[N_VEC:, :] = jnp.zeros((vec.shape[0] - N_VEC, D), F32)
    vec[11:12, :], vec[12:13, :], vec[10:11, :] = (total_row(s) for s in sums)

    acc[...] = d_res[...]

    def ffn_back(j, _):
        cols = at(j, D)
        acc2[...] = dot_nt(dmat[:, C_FB : C_FB + D], w_fo[cols, :])

        def inner(rs, i, c):
            d = (slope[rs, cols].astype(F32) * acc2[rs, :]).astype(BF)
            act[rs, :] = d
            return c + partial_rows(d.astype(F32))

        vec[pl.ds(13 + j, 1), :] = total_row(row_blocks(rows, 32, inner, zero))
        dmat[:, cols] = act[...]
        acc[...] += dot_nt(act[...], w_fi[:, cols])
        return 0

    lax.fori_loop(0, FF // D, ffn_back, 0)

    def ln2_back(rs, i, c):
        g, xhat = acc[rs, :], xhat2[rs, :]
        d = norm_rows_back(g, xhat, rstd2[rs, :], norm2[0:1, :])
        d_res[rs, :] = d
        db = d.astype(BF)
        dmat[rs, C_CB : C_CB + D] = db
        return (c[0] + partial_rows(g * xhat), c[1] + partial_rows(g), c[2] + partial_rows(db.astype(F32)))

    sums = row_blocks(rows, 32, ln2_back, (zero, zero, zero))
    vec[8:9, :], vec[9:10, :], vec[7:8, :] = (total_row(s) for s in sums)

    dmix[...] = dot_nt(dmat[:, C_CB : C_CB + D], w_co[...]).astype(BF)

    def put_store(j, dk, dv):
        dkv[:, at(j, 2 * HD)] = dk.astype(BF)
        dkv[:, pl.ds(pl.multiple_of(D + j * 2 * HD, 2 * HD), 2 * HD)] = dv.astype(BF)
        vec[pl.ds(6, 1), at(j, 2 * HD)] = total_row(dv)

    attend_back(p_c, dmix, cquery, sv, svt, dqt, put_store)
    dstore[...] = dot_nt(dkv[...], w_ckv[...]).astype(BF)
    dq = dqt[...].T
    dmat[:, C_CQ : C_CQ + D] = dq
    vec[5:6, :] = total_row(partial_rows(dq.astype(F32)))
    acc[...] = d_res[...] + dot_nt(dq, w_cq[...])

    def ln1_back(rs, i, c):
        g, xhat = acc[rs, :], xhat1[rs, :]
        d = norm_rows_back(g, xhat, rstd1[rs, :], norm1[0:1, :])
        d_res[rs, :] = d
        db = d.astype(BF)
        dmat[rs, C_SB : C_SB + D] = db
        return (c[0] + partial_rows(g * xhat), c[1] + partial_rows(g), c[2] + partial_rows(db.astype(F32)))

    sums = row_blocks(rows, 32, ln1_back, (zero, zero, zero))
    vec[3:4, :], vec[4:5, :], vec[2:3, :] = (total_row(s) for s in sums)

    dmix[...] = dot_nt(dmat[:, C_SB : C_SB + D], w_so[...]).astype(BF)

    def put_self(j, dk, dv):
        dvb = dv.astype(BF)
        dmat[:, pl.ds(pl.multiple_of(C_PROJ + D + j * 2 * HD, 2 * HD), 2 * HD)] = dk.astype(BF)
        dmat[:, pl.ds(pl.multiple_of(C_PROJ + 2 * D + j * 2 * HD, 2 * HD), 2 * HD)] = dvb
        vec[pl.ds(1, 1), at(j, 2 * HD)] = total_row(dvb.astype(F32))

    attend_back(p_s, dmix, q, v, vt, dqt, put_self)
    dq = dqt[...].T
    dmat[:, C_PROJ : C_PROJ + D] = dq
    vec[0:1, :] = total_row(partial_rows(dq.astype(F32)))
    d_hidden[...] = d_res[...] + dot_nt(dmat[:, C_PROJ : C_PROJ + 3 * D], w_qkv[...])


def run_layer(args, states_all):
    (hidden, store, retrieved, live, lengths, self_qkv, self_bias, self_out, self_out_bias, norm1, cross_q, cross_q_bias,
     cross_kv, cross_v_bias, cross_out, cross_out_bias, norm2, ffn_in, ffn_in_bias, ffn_out, ffn_out_bias, norm3, cotangent) = args
    rows, slots = hidden.shape[2], states_all.shape[0]
    shape = jax.ShapeDtypeStruct
    vmem, hbm, smem = (pl.BlockSpec(memory_space=m) for m in (pltpu.VMEM, pl.ANY, pltpu.SMEM))
    weights = (self_qkv, self_out, cross_q, cross_kv, cross_out, ffn_in, ffn_out)
    scratch = [pltpu.VMEM(w.shape, BF) for w in weights] + [pltpu.SemaphoreType.DMA((len(weights),))]
    wide = (rows, D)
    for dims, kind in [
        (wide, BF), (wide, BF), (wide, BF), ((D, rows), BF), ((rows, rows), F32), ((HEADS, rows, rows), BF),
        ((slots, D), BF), ((slots, D), BF), ((D, slots), BF), ((slots, rows), F32), ((HEADS, slots, rows), BF),
        (wide, BF), (wide, BF), (wide, BF), (wide, F32), (wide, F32), (wide, F32), (wide, F32), (wide, F32), (wide, F32),
        (wide, BF), (wide, BF), ((rows, FF), BF), (wide, F32), ((D, rows), BF), ((rows, 1), F32), ((rows, 1), F32),
    ]:
        scratch.append(pltpu.VMEM(dims, kind))
    return pl.pallas_call(
        layer_kernel,
        out_shape=(
            shape(wide, BF), shape(wide, F32), shape((R_ALL, rows), BF), shape((FF, rows), BF),
            shape((rows, C_ALL), BF), shape((slots, 2 * D), BF), shape((slots, D), BF), shape((24, D), F32),
        ),
        in_specs=[vmem] * 4 + [smem] + [vmem] * 11 + [hbm] * 7,
        out_specs=(vmem,) * 8,
        scratch_shapes=scratch,
        compiler_params=pltpu.CompilerParams(vmem_limit_bytes=VMEM_LIMIT),
        cost_estimate=pl.CostEstimate(flops=10**10, bytes_accessed=5 * 10**7, transcendentals=10**6),
    )(
        hidden[0, 0], states_all, retrieved[0, 0], live[0, 0], lengths, self_bias, self_out_bias, norm1, cross_q_bias,
        cross_v_bias, cross_out_bias, norm2, ffn_in_bias.reshape(FF // D, D), ffn_out_bias, norm3, cotangent[0, 0], *weights,
    )


def gather_kernel(n, states, whole, held, send_sem, recv_sem):
    me, rep = lax.axis_index("blk"), lax.axis_index("rep")
    barrier = pltpu.get_barrier_semaphore()
    for step in range(1, n):
        pl.semaphore_signal(barrier, inc=1, device_id=(lax.rem(me + step, n), rep), device_id_type=MESH)
    held[me] = states[...]
    pl.semaphore_wait(barrier, n - 1)
    copies = []
    for step in range(1, n):
        copies.append(
            pltpu.make_async_remote_copy(
                src_ref=states, dst_ref=held.at[me], send_sem=send_sem.at[step - 1], recv_sem=recv_sem.at[step - 1],
                device_id=(lax.rem(me + step, n), rep), device_id_type=MESH,
            )
        )
        copies[-1].start()
    for copy in copies:
        copy.wait()
    whole[...] = held[...]


def gather_states(states, n):
    block = states.shape
    vmem = pl.BlockSpec(memory_space=pltpu.VMEM)
    whole = pl.pallas_call(
        functools.partial(gather_kernel, n),
        out_shape=jax.ShapeDtypeStruct((n, *block), BF),
        in_specs=[vmem],
        out_specs=vmem,
        scratch_shapes=[pltpu.VMEM((n, *block), BF), pltpu.SemaphoreType.DMA((n - 1,)), pltpu.SemaphoreType.DMA((n - 1,))],
        compiler_params=pltpu.CompilerParams(collective_id=0, has_side_effects=True),
    )(states)
    return whole.reshape(n * block[0], block[1])


PART = 384
SHARD = D // 8
PAIRS = 8
PIECES = [("fo", i) for i in range(4)] + [("fi", i) for i in range(4)]
PIECES += [("co", 0), ("cq", 0), ("ckv", 0), ("ckv", 1), ("so", 0), ("qkv", 0), ("qkv", 1), ("qkv", 2)]
H_INNER, H_PROJ, H_SB, H_CQ, H_CB, H_FB, H_ALL = 0, 1536, 2688, 3072, 3456, 3840, 4608


def sum_kernel(
    xt, act_t, states, dmat, dkv, dstore, vec, fin_out, dstore_out, vec_out,
    xc, ac, sc, dc, dkc, l_sem, os_sem, or_sem,
    g, ax, hx, az, hz, ay, by, hy, bx, hbx, bz, fin,
    axs, axr, azs, azr, ays, ayr, bys, byr, bxs, bxr, bzs, bzr, bgs, bgr, cs, cr, f_sem,
    ds_in, vsh, vin, vrep, dss, dsr, vss, vsr, vps, vpr, v_sem,
):
    b, r = lax.axis_index("blk"), lax.axis_index("rep")
    z, x, y, c = b // 2, b % 2, r // 2, r % 2
    rows = dmat.shape[0]
    slots = states.shape[0]
    at_x = (z * 2 + 1 - x, r)
    at_y = (b, (1 - y) * 2 + c)
    at_c = (b, y * 2 + 1 - c)
    at_z = [(lax.rem(z + step, 4) * 2 + x, r) for step in range(1, 4)]
    at_blk = [(lax.rem(b + step, 8), r) for step in range(1, 8)]
    at_rep = [(b, lax.rem(r + step, 4)) for step in range(1, 4)]

    def send(src, dst, s_sem, r_sem, device):
        copy = pltpu.make_async_remote_copy(
            src_ref=src, dst_ref=dst, send_sem=s_sem, recv_sem=r_sem, device_id=device, device_id_type=MESH
        )
        copy.start()
        return copy

    barrier = pltpu.get_barrier_semaphore()
    for device in at_blk + at_rep:
        pl.semaphore_signal(barrier, inc=1, device_id=device, device_id_type=MESH)

    def halves(who):
        def cols(start, width):
            return pl.ds(pl.multiple_of(start + who * width, 128), width)

        return [
            (act_t.at[:, who], ac.at[:, :, 0:rows], ac.at[:, :, rows:]),
            (dmat.at[:, C_FB : C_FB + D], dc.at[0:rows, H_FB : H_FB + D], dc.at[rows:, H_FB : H_FB + D]),
            (xt.at[0:D], xc.at[0:D, 0:rows], xc.at[0:D, rows:]),
            (dmat.at[:, cols(C_INNER, 1536)], dc.at[0:rows, 0:1536], dc.at[rows:, 0:1536]),
            (xt.at[D:R_ALL], xc.at[D:R_ALL, 0:rows], xc.at[D:R_ALL, rows:]),
            (dmat.at[:, cols(C_PROJ, 1152)], dc.at[0:rows, H_PROJ:H_SB], dc.at[rows:, H_PROJ:H_SB]),
            (dmat.at[:, cols(C_SB, 384)], dc.at[0:rows, H_SB:H_CQ], dc.at[rows:, H_SB:H_CQ]),
            (dmat.at[:, cols(C_CQ, 384)], dc.at[0:rows, H_CQ:H_CB], dc.at[rows:, H_CQ:H_CB]),
            (dmat.at[:, cols(C_CB, 384)], dc.at[0:rows, H_CB:H_FB], dc.at[rows:, H_CB:H_FB]),
            (states, sc.at[0:slots], sc.at[slots:]),
            (dkv.at[:, cols(0, D)], dkc.at[0:slots], dkc.at[slots:]),
        ]

    mine, theirs = halves(c), halves(1 - c)
    local = []
    for i, (src, dst, _) in enumerate(mine):
        local.append(pltpu.make_async_copy(src, dst, l_sem.at[i]))
        local[-1].start()
    vsh[...] = jnp.zeros_like(vsh)
    for s in range(8):
        vsh[s, 0:13, 0:SHARD] = vec[0:13, s * SHARD : (s + 1) * SHARD]
        for part in range(4):
            begin = 384 * s + SHARD * part
            vsh[s, 13 + part : 14 + part, 0:SHARD] = vec[13 + begin // D : 14 + begin // D, begin % D : begin % D + SHARD]
    pl.semaphore_wait(barrier, len(at_blk) + len(at_rep))
    sent = []
    exchange = []
    for i, (src, _, dst) in enumerate(theirs):
        exchange.append(send(src, dst, os_sem.at[i], or_sem.at[i], at_c))
    sent += exchange
    small_d, small_v = [], []
    for i, device in enumerate(at_blk):
        small_d.append(send(dstore.at[device[0]], ds_in.at[i], dss.at[i], dsr.at[i], device))
        small_v.append(send(vsh.at[device[0]], vin.at[i], vss.at[i], vsr.at[i], device))
    sent += small_d + small_v

    arrived = [False] * len(mine)

    def need(*which):
        for i in which:
            if not arrived[i]:
                local[i].wait()
                exchange[i].wait_recv()
                arrived[i] = True

    def product(i):
        kind, part = PIECES[i]
        if kind == "fo":
            need(0, 1)
            left = ac[:, (part // 2) * SHARD : (part // 2 + 1) * SHARD, :].reshape(8 * SHARD, 2 * rows)
            right = dc[:, H_FB + (part % 2) * PART : H_FB + (part % 2 + 1) * PART]
        elif kind == "ckv":
            need(9, 10)
            left, right = sc[...].T, dkc[:, part * PART : (part + 1) * PART]
        else:
            uses, row, col = {
                "fi": ((2, 3), R_SECOND, H_INNER), "co": ((4, 8), R_CMIX, H_CB), "cq": ((4, 7), R_FIRST, H_CQ),
                "so": ((4, 6), R_SMIX, H_SB), "qkv": ((4, 5), R_TOK, H_PROJ),
            }[kind]
            need(*uses)
            left, right = xc[row : row + D, :], dc[:, col + part * PART : col + (part + 1) * PART]
        g[i] = dot(left, right).astype(BF).reshape(4, 2, 2, SHARD // 2, PART)

    steps_a = [[None] * PAIRS for _ in range(4)]
    steps_b = [[None] * PAIRS for _ in range(5)]

    def a0(t):
        product(2 * t)
        steps_a[0][t] = send(g.at[2 * t, :, 1 - x], ax.at[t], axs.at[t], axr.at[t], at_x)

    def a1(t):
        steps_a[0][t].wait_recv()
        hx[t] = g[2 * t, :, x] + ax[t]
        steps_a[1][t] = []
        for i, device in enumerate(at_z):
            steps_a[1][t].append(send(hx.at[t, device[0] // 2], az.at[t, i], azs.at[t, i], azr.at[t, i], device))

    def a2(t):
        for copy in steps_a[1][t]:
            copy.wait_recv()
        own, far = hx[t, z], az[t]
        hz[t] = ((own.astype(F32) + far[0].astype(F32)) + (far[1].astype(F32) + far[2].astype(F32))).astype(BF)
        steps_a[2][t] = send(hz.at[t], ay.at[t], ays.at[t], ayr.at[t], at_y)

    def finish(i):
        steps = steps_a[3] if i % 2 == 0 else steps_b[4]
        steps[i // 2] = send(fin.at[i, c], fin.at[i, c], cs.at[i], cr.at[i], at_c)

    def a3(t):
        steps_a[2][t].wait_recv()
        fin[2 * t, c] = hz[t] + ay[t]
        finish(2 * t)

    def b0(t):
        product(2 * t + 1)
        steps_b[0][t] = send(g.at[2 * t + 1, :, :, 1 - y], by.at[t], bys.at[t], byr.at[t], at_y)

    def b1(t):
        steps_b[0][t].wait_recv()
        hy[t] = g[2 * t + 1, :, :, y] + by[t]
        steps_b[1][t] = send(hy.at[t, :, 1 - x], bx.at[t], bxs.at[t], bxr.at[t], at_x)

    def b2(t):
        steps_b[1][t].wait_recv()
        hbx[t] = hy[t, :, x] + bx[t]
        steps_b[2][t] = []
        for i, device in enumerate(at_z):
            steps_b[2][t].append(send(hbx.at[t, device[0] // 2], bz.at[t, i], bzs.at[t, i], bzr.at[t, i], device))

    def b3(t):
        for copy in steps_b[2][t]:
            copy.wait_recv()
        own, far = hbx[t, z], bz[t]
        total = (own.astype(F32) + far[0].astype(F32)) + (far[1].astype(F32) + far[2].astype(F32))
        fin[2 * t + 1, c, y] = total.astype(BF)
        steps_b[3][t] = send(fin.at[2 * t + 1, c, y], fin.at[2 * t + 1, c, y], bgs.at[t], bgr.at[t], at_y)

    def b4(t):
        steps_b[3][t].wait_recv()
        finish(2 * t + 1)

    out = []

    def close(i):
        (steps_a[3] if i % 2 == 0 else steps_b[4])[i // 2].wait_recv()
        out.append(pltpu.make_async_copy(fin.at[i], fin_out.at[i], f_sem.at[i]))
        out[-1].start()

    small = []
    for tick in range(PAIRS + 6):
        for body, lag in (
            (a0, 0), (b0, 0), (a1, 1), (b1, 1), (a2, 2), (b2, 2), (a3, 3), (b3, 3), (b4, 4),
            (lambda t: close(2 * t), 4), (lambda t: close(2 * t + 1), 5),
        ):
            if 0 <= tick - lag < PAIRS:
                body(tick - lag)
        if tick == 2:
            total = dstore[b].astype(F32)
            for i, copy in enumerate(small_d):
                copy.wait_recv()
                total = total + ds_in[i].astype(F32)
            dstore_out[...] = total
            total = vsh[b]
            for i, copy in enumerate(small_v):
                copy.wait_recv()
                total = total + vin[i]
            vrep[r] = total
            for i, device in enumerate(at_rep):
                small.append(send(vrep.at[r], vrep.at[r], vps.at[i], vpr.at[i], device))
            sent += small
        if tick == 4:
            for copy in small:
                copy.wait_recv()
            vec_out[...] = (vrep[0] + vrep[1]) + (vrep[2] + vrep[3])
    for steps in steps_a + steps_b:
        for entry in steps:
            sent += entry if isinstance(entry, list) else [entry]
    for copy in sent:
        copy.wait_send()
    for copy in out:
        copy.wait()


def sum_gradients(states, xt, act_t, dmat, dkv, dstore, vec):
    rows, slots = dmat.shape[0], states.shape[0]
    n = len(PIECES)
    vmem, hbm = (pl.BlockSpec(memory_space=m) for m in (pltpu.VMEM, pl.ANY))
    shape = jax.ShapeDtypeStruct
    sem = lambda *dims: pltpu.SemaphoreType.DMA(dims)
    buf = lambda *dims: pltpu.VMEM(dims, BF)
    p = PAIRS
    half = SHARD // 2
    scratch = [
        buf(R_ALL, 2 * rows), buf(8, 2 * SHARD, 2 * rows), buf(2 * slots, D), buf(2 * rows, H_ALL), buf(2 * slots, D),
        sem(11), sem(11), sem(11),
        buf(n, 4, 2, 2, half, PART), buf(p, 4, 2, half, PART), buf(p, 4, 2, half, PART), buf(p, 3, 2, half, PART),
        buf(p, 2, half, PART), buf(p, 2, half, PART), buf(p, 4, 2, half, PART), buf(p, 4, 2, half, PART),
        buf(p, 4, half, PART), buf(p, 4, half, PART), buf(p, 3, half, PART), buf(n, 2, 2, half, PART),
        sem(p), sem(p), sem(p, 3), sem(p, 3), sem(p), sem(p), sem(p), sem(p), sem(p), sem(p), sem(p, 3), sem(p, 3),
        sem(p), sem(p), sem(n), sem(n), sem(n),
        buf(7, slots // 8, D), pltpu.VMEM((8, 24, 128), F32), pltpu.VMEM((7, 24, 128), F32), pltpu.VMEM((4, 24, 128), F32),
        sem(7), sem(7), sem(7), sem(7), sem(3), sem(3), sem(1),
    ]
    return pl.pallas_call(
        sum_kernel,
        out_shape=(shape((n, 2, 2, half, PART), BF), shape((slots // 8, D), F32), shape((24, 128), F32)),
        in_specs=[hbm] * 5 + [vmem] * 2,
        out_specs=(hbm, vmem, vmem),
        scratch_shapes=scratch,
        compiler_params=pltpu.CompilerParams(collective_id=1, has_side_effects=True, vmem_limit_bytes=VMEM_LIMIT),
        cost_estimate=pl.CostEstimate(flops=5 * 10**9, bytes_accessed=3 * 10**7, transcendentals=0),
    )(xt, act_t.reshape(8, 2, 2 * SHARD, rows), states, dmat, dkv, dstore.reshape(8, slots // 8, D), vec)


def place_kernel(fin, dstore, vec, *outs):
    (o_dstore, o_qkv, o_sbias, o_so, o_sob, o_n1, o_cq, o_cqb, o_ckv, o_cvb, o_co, o_cob, o_n2, o_fi, o_fib, o_fo, o_fob, o_n3) = outs
    o_dstore[...] = dstore[...]
    wide = {"qkv": o_qkv, "so": o_so, "cq": o_cq, "ckv": o_ckv, "co": o_co, "fi": o_fi}
    for i, (kind, part) in enumerate(PIECES):
        for c in range(2):
            values = fin[i, c].astype(F32)
            if kind == "fo":
                begin = c * 2 * SHARD + (part // 2) * SHARD
                o_fo[begin : begin + SHARD, (part % 2) * PART : (part % 2 + 1) * PART] = values
            else:
                ref = wide[kind]
                begin = c * (ref.shape[1] // 2) + part * PART
                ref[:, begin : begin + PART] = values
    for ref, row in ((o_sbias, 0), (o_n1, 3), (o_n2, 8), (o_n3, 11)):
        ref[...] = vec[row : row + 2, 0:SHARD]
    for ref, row in ((o_sob, 2), (o_cqb, 5), (o_cvb, 6), (o_cob, 7), (o_fob, 10)):
        ref[...] = vec[row, 0:SHARD]
    for part in range(4):
        o_fib[pl.ds(part * SHARD, SHARD)] = vec[13 + part, 0:SHARD]


def place(fin, dstore, vec):
    shape = lambda *dims: jax.ShapeDtypeStruct(dims, F32)
    return pl.pallas_call(
        place_kernel,
        out_shape=(
            shape(*dstore.shape), shape(SHARD, 3 * D), shape(2, SHARD), shape(SHARD, D), shape(SHARD), shape(2, SHARD),
            shape(SHARD, D), shape(SHARD), shape(SHARD, 2 * D), shape(SHARD), shape(SHARD, D), shape(SHARD), shape(2, SHARD),
            shape(SHARD, FF), shape(FF // 8), shape(FF // 8, D), shape(SHARD), shape(2, SHARD),
        ),
        compiler_params=pltpu.CompilerParams(vmem_limit_bytes=VMEM_LIMIT),
    )(fin.reshape(len(PIECES), 2, SHARD, PART), dstore, vec)


def sum_plainly(states, xt, act_t, dmat, dkv, dstore, vec):
    def total(value, dim):
        part = lax.psum_scatter(value, "blk", scatter_dimension=dim, tiled=True)
        return lax.psum(part.astype(BF), "rep").astype(F32)

    def rows_of(start):
        return lax.slice_in_dim(xt, start, start + D, axis=0)

    def cols_of(start, width):
        return lax.slice_in_dim(dmat, start, start + width, axis=1)

    g_qkv = total(dot(rows_of(R_TOK), cols_of(C_PROJ, 3 * D)), 0)
    g_so = total(dot(rows_of(R_SMIX), cols_of(C_SB, D)), 0)
    g_cq = total(dot(rows_of(R_FIRST), cols_of(C_CQ, D)), 0)
    g_co = total(dot(rows_of(R_CMIX), cols_of(C_CB, D)), 0)
    g_fi = total(dot(rows_of(R_SECOND), cols_of(C_INNER, FF)), 0)
    g_fo = total(dot(act_t, cols_of(C_FB, D)), 0)
    g_ckv = total(dot_tn(states, dkv), 0)
    g_store = lax.psum_scatter(dstore.astype(F32), "blk", scatter_dimension=0, tiled=True)
    g_fib = total(vec[13:N_VEC].reshape(FF), 0)
    v = total(vec[:13].T, 0)
    two = lambda row: v[:, row : row + 2].T
    return (
        g_store, g_qkv, two(0), g_so, v[:, 2], two(3), g_cq, v[:, 5], g_ckv, v[:, 6], g_co, v[:, 7], two(8),
        g_fi, g_fib, g_fo, v[:, 10], two(11),
    )


def on_device(fast, n, *args):
    states = args[1][0]
    states_all = gather_states(states, n) if fast else lax.all_gather(states, "blk", axis=0, tiled=True)
    result, d_hidden, *operands = run_layer(args, states_all)
    if fast:
        grads = place(*sum_gradients(states_all, *operands))
    else:
        grads = sum_plainly(states_all, *operands)
    return (result[None, None], d_hidden[None, None], grads[0][None], *grads[1:])


def solution(mesh):
    n = mesh.shape["blk"]
    fast = n == 8 and mesh.shape["rep"] == 4
    deep, flat = P("rep", "blk", None, None), P("rep", "blk", None)
    in_specs = (deep, flat, deep, deep, P("rep", "blk")) + (P(),) * 17 + (deep,)
    w, vec, two = P("blk", None), P("blk"), P(None, "blk")
    out_specs = (deep, deep, flat, w, two, w, vec, two, w, vec, w, vec, w, vec, two, w, vec, w, vec, two)
    return jax.shard_map(
        functools.partial(on_device, fast, n), mesh=mesh, in_specs=in_specs, out_specs=out_specs, check_vma=False
    )
```

```python
import functools
import typing

import jax
import jax.numpy as jnp
from jax import lax
from jax.experimental import pallas as pl
from jax.experimental.pallas import tpu as pltpu
from jax.sharding import PartitionSpec as P

D = 768
HEADS = 12
HD = 64
FF = 3072
EPS = 1e-05
NEG = -1e30
BF = jnp.bfloat16
F32 = jnp.float32
MESH = pl.DeviceIdType.MESH
VMEM_LIMIT = 63 * 2**20

N_VEC = 17
R_SECOND, R_TOK, R_SMIX, R_FIRST, R_CMIX, R_ALL = 0, 768, 1536, 2304, 3072, 3840
PART = 384
SHARD = D // 8
PIECES = [("fo", i) for i in range(4)] + [("fi", i) for i in range(4)]
PIECES += [("co", 0), ("cq", 0), ("ckv", 0), ("ckv", 1), ("so", 0), ("qkv", 0), ("qkv", 1), ("qkv", 2)]
OPERANDS = ["fb"] * 4 + ["inner0", "inner1", "inner2", "inner3", "cb", "cq", "dkv0", "dkv1", "sb", "proj0", "proj1", "proj2"]
WAYS = "BABACBCBBABBABAB"
ORDER = (
    0, 1, 2, 100, 101, 102, 103, 104, 105, 3, 4, 5, 6, 7, 106, 200, 8, 201, 107, 9, 10, 11, 108, 204,
    202, 12, 203, 13, 14, 15, 16, 109, 300, 110, 205, 17, 302, 112, 18, 206, 19, 111, 304, 207, 20, 209, 301, 21,
    22, 305, 114, 115, 303, 208, 400, 306, 212, 402, 113, 401, 404, 23, 210, 403, 500, 307, 309, 502, 405, 211, 214, 409,
    312, 505, 308, 24, 407, 215, 406, 412, 310, 314, 507, 213, 408, 311, 501, 410, 504, 315, 503, 414, 411, 600, 508, 602,
    510, 313, 509, 415, 605, 511, 506, 413, 512, 515, 607, 514, 608, 513, 610, 611, 615, 613,
)
O_INNER, O_PROJ, O_SB, O_CQ, O_CB, O_FB, O_ALL = 0, 1536, 2688, 3072, 3456, 3840, 4608


class Columns(typing.NamedTuple):
    inner: int
    proj: int
    sb: int
    cq: int
    cb: int
    fb: int
    end: int


def columns(fast):
    return Columns(0, 0, 2304, 3072, 3840, 4608, 5376) if fast else Columns(0, 3072, 5376, 6144, 6912, 7680, 8448)


def dot(a, b):
    return lax.dot_general(a, b, (((1,), (0,)), ((), ())), preferred_element_type=F32)


def dot_nt(a, b):
    return lax.dot_general(a, b, (((1,), (1,)), ((), ())), preferred_element_type=F32)


def dot_tn(a, b):
    return lax.dot_general(a, b, (((0,), (0,)), ((), ())), preferred_element_type=F32)


def at(index, size):
    return pl.ds(pl.multiple_of(index * size, size), size)


def half_mask(half):
    lane = lax.broadcasted_iota(jnp.int32, (1, 2 * HD), 1)
    return ((lane >= HD) if half else (lane < HD)).astype(F32).astype(BF)


def total_row(values):
    return jnp.sum(values, axis=0, keepdims=True)


def gelu_and_slope(v):
    cdf = 0.5 * (1.0 + lax.erf(v * 0.7071067811865476))
    return v * cdf, cdf + v * (jnp.exp(-0.5 * v * v) * 0.3989422804014327)


def norm_rows(r):
    centered = r - jnp.mean(r, axis=-1, keepdims=True)
    rstd = lax.rsqrt(jnp.mean(centered * centered, axis=-1, keepdims=True) + EPS)
    return centered * rstd, rstd


def norm_rows_back(grad, xhat, rstd, gain):
    e = grad * gain
    mean_e = jnp.mean(e, axis=-1, keepdims=True)
    mean_x = jnp.mean(e * xhat, axis=-1, keepdims=True)
    return (e - mean_e - xhat * mean_x) * rstd


def attend(q_ref, k_ref, vt_ref, bias_ref, p_ref, mix_t_ref):
    scores = []
    for j in range(HEADS // 2):
        cols = slice(2 * HD * j, 2 * HD * (j + 1))
        q2, k2 = q_ref[:, cols], k_ref[:, cols]
        scores += [dot_nt(k2 * half_mask(half), q2) for half in range(2)]
    for h, st in enumerate(scores):
        st = st + bias_ref[...]
        e = jnp.exp(st - jnp.max(st, axis=0, keepdims=True))
        p_ref[h] = (e * (1.0 / jnp.sum(e, axis=0, keepdims=True))).astype(BF)
    for h in range(HEADS):
        rows = slice(HD * h, HD * (h + 1))
        mix_t_ref[rows, :] = dot(vt_ref[rows, :], p_ref[h]).astype(BF)


def attend_back(p_ref, dmix_ref, q_ref, v_ref, kt_ref, dq_t_ref, put, begin, end):
    parts = []
    for j in range(begin, end):
        cols = slice(2 * HD * j, 2 * HD * (j + 1))
        dm2, q2, v2 = dmix_ref[:, cols], q_ref[:, cols], v_ref[:, cols]
        parts += [(2 * j + half, dm2 * half_mask(half), q2 * half_mask(half), dot_nt(v2 * half_mask(half), dm2)) for half in range(2)]
    grads = []
    for h, dm, q, dp in parts:
        p = p_ref[h].astype(F32)
        t = p * dp
        grads.append((t - p * jnp.sum(t, axis=0, keepdims=True)).astype(BF))
    for n, (h, dm, q, dp) in enumerate(parts):
        dq_t_ref[HD * h : HD * (h + 1), :] = dot(kt_ref[HD * h : HD * (h + 1), :], grads[n]).astype(BF)
    for n in range(0, len(parts), 2):
        (h, dm0, q0, _), (_, dm1, q1, _) = parts[n : n + 2]
        put(h // 2, dot(grads[n], q0) + dot(grads[n + 1], q1), dot(p_ref[h], dm0) + dot(p_ref[h + 1], dm1))


class Refs:
    def __init__(self, names, refs):
        for name, ref in zip(names, refs, strict=True):
            setattr(self, name, ref)


class Inputs(typing.NamedTuple):
    tokens: typing.Any
    states: typing.Any
    retrieved: typing.Any
    live: typing.Any
    lengths: typing.Any
    self_bias: typing.Any
    self_out_bias: typing.Any
    norm1: typing.Any
    cq_bias: typing.Any
    cv_bias: typing.Any
    co_bias: typing.Any
    norm2: typing.Any
    fi_bias: typing.Any
    fo_bias: typing.Any
    norm3: typing.Any
    cotangent: typing.Any
    h_qkv: typing.Any
    h_qkv6: typing.Any
    h_so: typing.Any
    h_cq: typing.Any
    h_ckv: typing.Any
    h_co: typing.Any
    h_fi: typing.Any
    h_fo: typing.Any


INPUTS = list(Inputs._fields)


def layer(m, net, at_col):
    rows = m.tokens.shape[0]
    length = m.lengths[0, 0]
    scale = HD**-0.5
    xt, dmat, vec = m.xt, m.dmat, m.vec
    copies = {}
    order = [("qkv%d" % i, m.h_qkv6.at[:, :, :, :, i * PART : (i + 1) * PART], m.ring.at[i]) for i in range(6)]
    order += [("so", m.h_so, m.w_so), ("cq", m.h_cq, m.w_cq), ("ckv", m.h_ckv, m.w_ckv), ("co", m.h_co, m.w_co)]
    order += [("fi", m.h_fi, m.w_fi), ("fo", m.h_fo, m.w_fo)]
    for i, (name, src, dst) in enumerate(order):
        copies[name] = pltpu.make_async_copy(src, dst, m.w_sem.at[i])
        copies[name].start()
    if net:
        net.greet()

    def piece(name):
        return slice(getattr(at_col, name), getattr(at_col, name) + D)

    xt[R_TOK : R_TOK + D, :] = m.tokens[...].T
    key_at = lax.broadcasted_iota(jnp.int32, (rows, rows), 0)
    query_at = lax.broadcasted_iota(jnp.int32, (rows, rows), 1)
    m.bias_s[...] = jnp.where((key_at <= query_at) & (key_at < length), 0.0, NEG)
    if net:
        net.begin()
    topk = m.retrieved.shape[0]
    slots = m.bias_c.shape[0]
    slot_rank = lax.broadcasted_iota(jnp.int32, (topk, rows), 0)
    chosen = jnp.where((m.live[...] > 0) | (slot_rank == 0), m.retrieved[...], -1)

    def mask_rows(i, _):
        ids = lax.broadcasted_iota(jnp.int32, (32, rows), 0) + i * 32
        hit = jnp.zeros((32, rows), jnp.bool_)
        for j in range(topk):
            hit = hit | (ids == chosen[j : j + 1, :])
        m.bias_c[at(i, 32), :] = jnp.where(hit, 0.0, NEG)
        return 0

    lax.fori_loop(0, slots // 32, mask_rows, 0)

    for i, (ref, bias) in enumerate(((m.q, 0), (m.q, 0), (m.k, None), (m.k, None), (m.v, 1), (m.v, 1))):
        copies["qkv%d" % i].wait()
        cols = slice((i % 2) * PART, (i % 2 + 1) * PART)
        got = dot(m.tokens[...], m.ring[i].reshape(D, PART))
        if bias is not None:
            got = got + m.self_bias[bias : bias + 1, cols]
        got = got.astype(BF)
        ref[:, cols] = got * scale if bias == 0 else got
    m.vt[...] = m.v[...].T
    attend(m.q, m.k, m.vt, m.bias_s, m.p_s, xt.at[R_SMIX : R_SMIX + D])
    m.vt[...] = m.k[...].T * scale
    copies["so"].wait()
    if net:
        net.swap_rows("smix")
    m.mix_b[...] = xt[R_SMIX : R_SMIX + D, :].T
    m.acc[...] = dot(m.mix_b[...], m.w_so[...])

    def ln1(rs):
        xhat, rstd = norm_rows(m.tokens[rs, :].astype(F32) + m.acc[rs, :] + m.self_out_bias[...][None, :])
        m.xhat1[rs, :] = xhat
        m.rstd1[rs, :] = rstd
        m.sec_b[rs, :] = (xhat * m.norm1[0:1, :] + m.norm1[1:2, :]).astype(BF)

    ln1(slice(0, rows))
    xt[R_FIRST : R_FIRST + D, :] = m.sec_b[...].T
    if net:
        net.swap_rows("first")

    copies["cq"].wait()
    m.k[...] = (dot(m.sec_b[...], m.w_cq[...]) + m.cq_bias[...][None, :]).astype(BF) * scale
    copies["ckv"].wait()
    if net:
        net.have_states()
    states = m.all_states[...].reshape(slots, D)
    m.sk[...] = dot(states, m.w_ckv[:, :D]).astype(BF)
    m.sv[...] = (dot(states, m.w_ckv[:, D:]) + m.cv_bias[...][None, :]).astype(BF)
    m.svt[...] = m.sv[...].T
    attend(m.k, m.sk, m.svt, m.bias_c, m.p_c, xt.at[R_CMIX : R_CMIX + D])
    m.svt[...] = m.sk[...].T * scale
    copies["co"].wait()
    if net:
        net.swap_rows("cmix")
    m.mix_b[...] = xt[R_CMIX : R_CMIX + D, :].T
    m.acc[...] = dot(m.mix_b[...], m.w_co[...])

    def ln2(rs):
        first = m.xhat1[rs, :] * m.norm1[0:1, :] + m.norm1[1:2, :]
        xhat, rstd = norm_rows(first + m.acc[rs, :] + m.co_bias[...][None, :])
        m.xhat2[rs, :] = xhat
        m.rstd2[rs, :] = rstd
        m.sec_b[rs, :] = (xhat * m.norm2[0:1, :] + m.norm2[1:2, :]).astype(BF)

    ln2(slice(0, rows))
    xt[R_SECOND : R_SECOND + D, :] = m.sec_b[...].T
    if net:
        net.swap_rows("second")

    copies["fi"].wait()
    copies["fo"].wait()
    for j in range(FF // D):
        cols = slice(j * D, (j + 1) * D)
        m.acc2[...] = dot(m.sec_b[...], m.w_fi[:, cols])
        bias = m.fi_bias[cols][None, :]

        def gelu(rs):
            a, s = gelu_and_slope(m.acc2[rs, :] + bias)
            m.mix_b[rs, :] = a.astype(BF)
            m.slope[rs, cols] = s.astype(BF)

        gelu(slice(0, rows))
        m.act_t[2 * j : 2 * j + 2] = m.mix_b[...].T.reshape(2, 2, 2 * SHARD, rows)
        if net:
            net.swap_act(j)
        got = dot(m.mix_b[...], m.w_fo[cols, :])
        m.acc[...] = got if j == 0 else m.acc[...] + got

    def ln3(rs):
        second = m.xhat2[rs, :] * m.norm2[0:1, :] + m.norm2[1:2, :]
        xhat, rstd = norm_rows(second + m.acc[rs, :] + m.fo_bias[...][None, :])
        m.result[rs, :] = (xhat * m.norm3[0:1, :] + m.norm3[1:2, :]).astype(BF)
        place = lax.broadcasted_iota(jnp.int32, (rows, 1), 0)
        g = m.cotangent[rs, :].astype(F32) * jnp.where(place < length, 1.0, 0.0)
        d = norm_rows_back(g, xhat, rstd, m.norm3[0:1, :])
        m.d_res[rs, :] = d
        db = d.astype(BF)
        dmat[rs, piece("fb")] = db
        return total_row(g * xhat), total_row(g), total_row(db.astype(F32))

    vec[N_VEC:, :] = jnp.zeros((vec.shape[0] - N_VEC, D), F32)
    vec[11:12, :], vec[12:13, :], vec[10:11, :] = ln3(slice(0, rows))
    if net:
        net.swap("fb")

    steps = []

    def feed_back(j):
        cols = slice(j * D, (j + 1) * D)
        inner = slice(at_col.inner + j * D, at_col.inner + (j + 1) * D)
        m.acc2[...] = dot_nt(dmat[:, piece("fb")], m.w_fo[cols, :])

        def inner_rows(rs):
            d = (m.slope[rs, cols].astype(F32) * m.acc2[rs, :]).astype(BF)
            dmat[rs, inner] = d
            return total_row(d.astype(F32))

        vec[13 + j : 14 + j, :] = inner_rows(slice(0, rows))
        if net:
            net.swap("inner%d" % j)

    def feed_back_x(j):
        inner = slice(at_col.inner + j * D, at_col.inner + (j + 1) * D)
        got = dot_nt(dmat[:, inner], m.w_fi[:, j * D : (j + 1) * D])
        m.acc[...] = (m.d_res[...] if j == 0 else m.acc[...]) + got

    for j in range(FF // D):
        steps += [functools.partial(feed_back, j), functools.partial(feed_back_x, j)]

    def norm_back(xhat_ref, rstd_ref, norm, name):
        def block(rs):
            g, xhat = m.acc[rs, :], xhat_ref[rs, :]
            d = norm_rows_back(g, xhat, rstd_ref[rs, :], norm[0:1, :])
            m.d_res[rs, :] = d
            db = d.astype(BF)
            dmat[rs, piece(name)] = db
            return total_row(g * xhat), total_row(g), total_row(db.astype(F32))

        sums = block(slice(0, rows))
        if net:
            net.swap(name)
        return sums

    def back_norm2():
        copies["qkv"] = pltpu.make_async_copy(m.h_qkv, m.w_fi.at[:, 0 : 3 * D], m.w_sem.at[len(order)])
        copies["qkv"].start()
        vec[8:9, :], vec[9:10, :], vec[7:8, :] = norm_back(m.xhat2, m.rstd2, m.norm2, "cb")

    def back_cross_out():
        m.mix_b[...] = dot_nt(dmat[:, piece("cb")], m.w_co[...]).astype(BF)

    def put_store(j, dk, dv):
        cols = slice(2 * HD * j, 2 * HD * (j + 1))
        m.dkv[:, cols] = dk.astype(BF)
        m.dkv[:, D + 2 * HD * j : D + 2 * HD * (j + 1)] = dv.astype(BF)
        vec[6:7, cols] = total_row(dv)

    def back_cross(part):
        attend_back(m.p_c, m.mix_b, m.k, m.sv, m.svt, m.dqt, put_store, 2 * part, 2 * part + 2)
        if net and part == 2:
            net.swap("dkv0")
            net.swap("dkv1")

    def back_query():
        dq = m.dqt[...].T
        dmat[:, piece("cq")] = dq
        if net:
            net.swap("cq")
        vec[5:6, :] = total_row(dq.astype(F32))

    def back_store():
        m.dstore[...] = dot_nt(m.dkv[...], m.w_ckv[...]).astype(BF).reshape(m.dstore.shape)
        if net:
            net.send_dstore()

    def back_first():
        m.acc[...] = m.d_res[...] + dot_nt(dmat[:, piece("cq")], m.w_cq[...])

    def back_norm1():
        if net:
            net.inner_gone()
        vec[3:4, :], vec[4:5, :], vec[2:3, :] = norm_back(m.xhat1, m.rstd1, m.norm1, "sb")

    def back_self_out():
        m.mix_b[...] = dot_nt(dmat[:, piece("sb")], m.w_so[...]).astype(BF)

    def put_self(j, dk, dv):
        dvb = dv.astype(BF)
        begin = at_col.proj + D + 2 * HD * j
        dmat[:, begin : begin + 2 * HD] = dk.astype(BF)
        dmat[:, begin + D : begin + D + 2 * HD] = dvb
        vec[1:2, 2 * HD * j : 2 * HD * (j + 1)] = total_row(dvb.astype(F32))

    def back_self(part):
        attend_back(m.p_s, m.mix_b, m.q, m.v, m.vt, m.dqt, put_self, 2 * part, 2 * part + 2)
        if net and part == 2:
            net.swap("proj1")
            net.swap("proj2")

    def back_proj():
        dq = m.dqt[...].T
        dmat[:, at_col.proj : at_col.proj + D] = dq
        if net:
            net.swap("proj0")
        vec[0:1, :] = total_row(dq.astype(F32))
        if net:
            net.send_vec()

    def back_hidden():
        copies["qkv"].wait()
        m.acc[...] = m.d_res[...] + dot_nt(dmat[:, at_col.proj : at_col.proj + 3 * D], m.w_fi[:, 0 : 3 * D])
        if net:
            net.keep(m.acc, m.d_hidden)
            net.keep(m.result, m.result_out)

    steps += [back_norm2, back_cross_out] + [functools.partial(back_cross, part) for part in range(3)]
    steps += [back_query, back_store, back_first, back_norm1, back_self_out] + [functools.partial(back_self, part) for part in range(3)]
    steps += [back_proj, back_hidden]
    if net:
        steps += [net.small_sums, net.small_total]
        for number in ORDER:
            if number < 100:
                steps[number]()
            else:
                net.step(number // 100 - 1, number % 100)
        net.finish()
    else:
        for step in steps:
            step()


def weight_inputs(args):
    self_qkv, self_out, cross_q, cross_kv, cross_out, ffn_in, ffn_out = (args[i] for i in (5, 7, 10, 12, 14, 17, 19))
    return (self_qkv, self_qkv.reshape(4, 2, 2, D // 16, 3 * D), self_out, cross_q, cross_kv, cross_out, ffn_in, ffn_out)


def small_inputs(args):
    (hidden, store, retrieved, live, lengths, _, self_bias, _, self_out_bias, norm1, _, cross_q_bias,
     _, cross_v_bias, _, cross_out_bias, norm2, _, ffn_in_bias, _, ffn_out_bias, norm3, cotangent) = args
    return (
        hidden[0, 0], store[0], jnp.swapaxes(retrieved[0, 0], 0, 1), jnp.swapaxes(live[0, 0], 0, 1), lengths, self_bias,
        self_out_bias, norm1, cross_q_bias, cross_v_bias, cross_out_bias, norm2, ffn_in_bias, ffn_out_bias, norm3, cotangent[0, 0],
    )


def layer_scratch(rows, slots, ring):
    wide = (rows, D)
    return dict(
        ring=((ring, 4, 2, 2, D // 16, PART), BF), w_so=((D, D), BF), w_cq=((D, D), BF), w_ckv=((D, 2 * D), BF),
        w_co=((D, D), BF), w_fi=((D, FF), BF), w_fo=((FF, D), BF),
        q=(wide, BF), k=(wide, BF), v=(wide, BF), vt=((D, rows), BF), bias_s=((rows, rows), F32),
        p_s=((HEADS, rows, rows), BF), sk=((slots, D), BF), sv=((slots, D), BF), svt=((D, slots), BF),
        bias_c=((slots, rows), F32), p_c=((HEADS, slots, rows), BF), mix_b=(wide, BF),
        acc=(wide, F32), acc2=(wide, F32), xhat1=(wide, F32), xhat2=(wide, F32),
        sec_b=(wide, BF), slope=((rows, FF), BF), d_res=(wide, F32), dqt=((D, rows), BF),
        rstd1=((rows, 1), F32), rstd2=((rows, 1), F32),
    )


def buffers(table):
    return [pltpu.VMEM(dims, kind) for dims, kind in table.values()]


PLAIN_OUT = ["result", "acc", "xt", "act_t", "dmat", "dkv", "dstore", "vec"]


def plain_kernel(names, *refs):
    layer(Refs(names, refs), None, columns(False))


def run_plain(args, states_all):
    rows, slots = args[0].shape[2], states_all.shape[0]
    at_col = columns(False)
    table = layer_scratch(rows, slots, 6)
    del table["acc"]
    vmem, hbm, smem = (pl.BlockSpec(memory_space=s) for s in (pltpu.VMEM, pl.ANY, pltpu.SMEM))
    shape = jax.ShapeDtypeStruct
    names = INPUTS + PLAIN_OUT + list(table) + ["w_sem"]
    names[names.index("states")] = "all_states"
    small = small_inputs(args)
    outs = pl.pallas_call(
        functools.partial(plain_kernel, names),
        out_shape=(
            shape((rows, D), BF), shape((rows, D), F32), shape((R_ALL, rows), BF), shape((8, 2, 2 * SHARD, rows), BF),
            shape((rows, at_col.end), BF), shape((slots, 2 * D), BF), shape((slots, D), BF), shape((24, D), F32),
        ),
        in_specs=[vmem] * 4 + [smem] + [vmem] * 11 + [hbm] * 8,
        out_specs=(vmem,) * 8,
        scratch_shapes=buffers(table) + [pltpu.SemaphoreType.DMA((13,))],
        compiler_params=pltpu.CompilerParams(vmem_limit_bytes=VMEM_LIMIT),
    )(small[0], states_all, *small[2:], *weight_inputs(args))
    return outs


class Net:
    def __init__(self, m, at_col):
        self.m, self.at_col = m, at_col
        b, r = lax.axis_index("blk"), lax.axis_index("rep")
        self.b, self.r = b, r
        self.z, self.x, self.y, self.c = b // 2, b % 2, r // 2, r % 2
        z, x, y, c = self.z, self.x, self.y, self.c
        self.at_x = (z * 2 + 1 - x, r)
        self.at_y = (b, (1 - y) * 2 + c)
        self.at_c = (b, y * 2 + 1 - c)
        side = z // 2
        self.side, self.is_end = side, jnp.logical_or(z == 0, z == 3)
        self.at_mid, self.at_end = ((1 + side) * 2 + x, r), (3 * side * 2 + x, r)
        self.at_near, self.at_far = ((2 - side) * 2 + x, r), (3 * (1 - side) * 2 + x, r)
        self.at_blk = [(lax.rem(b + step, 8), r) for step in range(1, 8)]
        self.at_rep = [(b, lax.rem(r + step, 4)) for step in range(1, 4)]
        self.swaps, self.swap_count = {}, 0
        self.steps = {}
        self.sent, self.sent_end, self.sent_mid, self.locals, self.here = [], [], [], [], []
        self.cores = {i: [] for i in range(len(PIECES))}
        self.nth = {i: WAYS[:i].count(way) for i, way in enumerate(WAYS)}

    def copy(self, src, dst, s_sem, r_sem, device):
        return pltpu.make_async_remote_copy(
            src_ref=src, dst_ref=dst, send_sem=s_sem, recv_sem=r_sem, device_id=device, device_id_type=MESH
        )

    def send(self, *args):
        copy = self.copy(*args)
        copy.start()
        self.sent.append(copy)
        return copy

    def send_some(self, among, make):
        make().start()
        among.append(make)

    def greet(self):
        barrier = pltpu.get_barrier_semaphore()
        for device in self.at_blk + self.at_rep:
            pl.semaphore_signal(barrier, inc=1, device_id=device, device_id_type=MESH)

    def begin(self):
        m = self.m
        m.all_states[self.b] = m.states[...]
        pl.semaphore_wait(pltpu.get_barrier_semaphore(), len(self.at_blk) + len(self.at_rep))
        self.gather = []
        for i, device in enumerate(self.at_blk):
            self.gather.append(self.send(m.states, m.all_states.at[self.b], m.gs.at[i], m.gr.at[i], device))
        self.swap_rows("tok")

    def have_states(self):
        for copy in self.gather:
            copy.wait_recv()
        self.trade("states", self.m.all_states, self.m.states_p)

    def trade(self, name, src, dst):
        i = self.swap_count
        self.swap_count += 1
        self.swaps[name] = self.send(src, dst, self.m.os.at[i], self.m.orr.at[i], self.at_c)

    def need(self, *names):
        for name in names:
            if name not in self.here:
                self.swaps[name].wait_recv()
                self.here.append(name)

    def swap_rows(self, name):
        row = {"tok": R_TOK, "smix": R_SMIX, "first": R_FIRST, "cmix": R_CMIX, "second": R_SECOND}[name]
        self.trade(name, self.m.xt.at[row : row + D], self.m.xt_p.at[row : row + D])

    def swap_act(self, j):
        here = slice(2 * j, 2 * j + 2)
        self.trade("act%d" % j, self.m.act_t.at[here, 1 - self.c], self.m.act_p.at[here])

    def half(self, start, who):
        return pl.ds(pl.multiple_of(start + who * PART, 128), PART)

    def operand(self, name):
        m, at_col = self.m, self.at_col
        if name[:3] == "dkv":
            return m.dkv, int(name[3]) * D, m.dkv_p, int(name[3]) * PART
        if name[:5] == "inner":
            return m.dmat, at_col.inner + int(name[5]) * D, m.d_p, O_INNER + int(name[5]) * PART
        if name[:4] == "proj":
            return m.dmat, at_col.proj + int(name[4]) * D, m.d_p, O_PROJ + int(name[4]) * PART
        return m.dmat, getattr(at_col, name), m.d_p, {"sb": O_SB, "cq": O_CQ, "cb": O_CB}[name]

    def swap(self, name):
        m = self.m
        if name == "fb":
            start = self.at_col.fb
            self.trade("fb", m.dmat.at[:, start : start + D], m.d_p.at[:, O_FB : O_FB + D])
            return
        ref, start, there, place = self.operand(name)
        self.trade(name, ref.at[:, self.half(start, 1 - self.c)], there.at[:, place : place + PART])

    def product(self, i):
        m = self.m
        kind, part = PIECES[i]
        if kind == "fo":
            self.need("fb", *("act%d" % j for j in range(4)))
            up = slice((part // 2) * SHARD, (part // 2 + 1) * SHARD)
            left = m.act_t[:, self.c, up, :].reshape(D, -1)
            left_p = m.act_p[:, up, :].reshape(D, -1)
            begin = (part % 2) * PART
            right = m.dmat[:, self.at_col.fb + begin : self.at_col.fb + begin + PART]
            right_p = m.d_p[:, O_FB + begin : O_FB + begin + PART]
        else:
            name = OPERANDS[i]
            ref, start, there, place = self.operand(name)
            rows_of, row = {"fi": ("second", R_SECOND), "co": ("cmix", R_CMIX), "cq": ("first", R_FIRST), "ckv": ("states", 0),
                            "so": ("smix", R_SMIX), "qkv": ("tok", R_TOK)}[kind]
            self.need(rows_of, name)
            right = ref[:, self.half(start, self.c)]
            right_p = there[:, place : place + PART]
            if kind == "ckv":
                left = m.all_states[...].reshape(-1, D).T
                left_p = m.states_p[...].reshape(-1, D).T
            else:
                left, left_p = m.xt[row : row + D, :], m.xt_p[row : row + D, :]
        m.ring[i] = (dot(left, right) + dot(left_p, right_p)).astype(BF).reshape(4, 2, 2, SHARD // 2, PART)

    def step(self, stage, i):
        n = self.nth[i]
        if stage == 0:
            self.product(i)
        ways = {
            "A": (self.a0, self.a1, self.a2, self.a3, self.a4),
            "B": (self.b0, self.b1, self.b2, self.b3, self.b4, self.b5),
            "C": (self.c0, self.c1, self.c2, self.c3, self.c4),
        }
        ways[WAYS[i]][stage](i, n)

    def post(self, i, src, dst, device):
        n = len(self.steps.setdefault(i, []))
        self.steps[i].append(self.send(src, dst, self.m.ps.at[i, n], self.m.pr.at[i, n], device))

    def arrived(self, i):
        self.steps[i][-1].wait_recv()

    def z_send(self, i, part, zb):
        m, others, edge = self.m, pl.ds(1 - self.side, 3), 3 * self.side

        @pl.when(self.is_end)
        def _():
            self.send_some(self.sent_end, lambda: self.copy(part.at[others], zb, m.zs.at[i, 0], m.zr.at[i, 0], self.at_mid))

        @pl.when(jnp.logical_not(self.is_end))
        def _():
            self.send_some(self.sent_mid, lambda: self.copy(part.at[edge], zb.at[0], m.zs.at[i, 0], m.zr.at[i, 1], self.at_end))

    def z_pass(self, i, part, zb, zm):
        m, side = self.m, self.side
        others, far, near = pl.ds(1 - side, 3), 2 * (1 - side), 1

        @pl.when(jnp.logical_not(self.is_end))
        def _():
            self.copy(part.at[others], zb, m.zs.at[i, 0], m.zr.at[i, 0], self.at_end).wait_recv()
            zb[far] = zb[far] + part[3 * (1 - side)]
            self.send_some(self.sent_mid, lambda: self.copy(zb.at[far], zb.at[1], m.zs.at[i, 1], m.zr.at[i, 2], self.at_far))
            zb[near] = zb[near] + part[2 - side]
            self.send_some(self.sent_mid, lambda: self.copy(zb.at[near], zm, m.zs.at[i, 2], m.zr.at[i, 3], self.at_near))

    def z_sum(self, i, part, zb, zm, out):
        m, side = self.m, self.side

        @pl.when(self.is_end)
        def _():
            self.copy(part.at[0], zb.at[0], m.zs.at[i, 0], m.zr.at[i, 1], self.at_mid).wait_recv()
            self.copy(part.at[0], zb.at[1], m.zs.at[i, 0], m.zr.at[i, 2], self.at_near).wait_recv()
            out[...] = (part[self.z].astype(F32) + zb[0].astype(F32) + zb[1].astype(F32)).astype(BF)

        @pl.when(jnp.logical_not(self.is_end))
        def _():
            self.copy(part.at[0], zm, m.zs.at[i, 0], m.zr.at[i, 3], self.at_near).wait_recv()
            out[...] = (part[self.z].astype(F32) + zb[2 * side].astype(F32) + zm[...].astype(F32)).astype(BF)

    def last(self, i, ref, there):
        self.keep(ref, there)
        n = len(self.cores[i])
        self.cores[i].append(self.send(ref, there, self.m.cs.at[i, n], self.m.cr.at[i, n], self.at_c))

    def a0(self, i, n):
        self.post(i, self.m.ring.at[i, :, 1 - self.x], self.m.ax.at[n], self.at_x)

    def a1(self, i, n):
        m = self.m
        self.arrived(i)
        m.ax[n] = m.ax[n] + m.ring[i, :, self.x]
        self.z_send(i, m.ax.at[n], m.azb.at[n])

    def a2(self, i, n):
        self.z_pass(i, self.m.ax.at[n], self.m.azb.at[n], self.m.azm.at[n])

    def a3(self, i, n):
        m = self.m
        self.z_sum(i, m.ax.at[n], m.azb.at[n], m.azm.at[n], m.ah.at[n])
        self.post(i, m.ah.at[n], m.ay.at[n], self.at_y)

    def a4(self, i, n):
        m = self.m
        self.arrived(i)
        m.ay[n] = m.ay[n] + m.ah[n]
        self.last(i, m.ay.at[n], m.fin.at[i, self.c])

    def b0(self, i, n):
        self.post(i, self.m.ring.at[i, :, :, 1 - self.y], self.m.by.at[n], self.at_y)

    def b1(self, i, n):
        m = self.m
        self.arrived(i)
        m.by[n] = m.by[n] + m.ring[i, :, :, self.y]
        self.post(i, m.by.at[n, :, 1 - self.x], m.bx.at[n], self.at_x)

    def b2(self, i, n):
        m = self.m
        self.arrived(i)
        m.bx[n] = m.bx[n] + m.by[n, :, self.x]
        self.z_send(i, m.bx.at[n], m.bzb.at[n])

    def b3(self, i, n):
        self.z_pass(i, self.m.bx.at[n], self.m.bzb.at[n], self.m.bzm.at[n])

    def b4(self, i, n):
        m = self.m
        self.z_sum(i, m.bx.at[n], m.bzb.at[n], m.bzm.at[n], m.bh.at[n])
        self.post(i, m.bh.at[n], m.bg.at[n], self.at_y)
        self.last(i, m.bh.at[n], m.fin.at[i, self.c, self.y])

    def b5(self, i, n):
        self.arrived(i)
        self.last(i, self.m.bg.at[n], self.m.fin.at[i, self.c, 1 - self.y])

    def c0(self, i, n):
        self.z_send(i, self.m.ring.at[i], self.m.czb.at[n])

    def c1(self, i, n):
        self.z_pass(i, self.m.ring.at[i], self.m.czb.at[n], self.m.czm.at[n])

    def c2(self, i, n):
        m = self.m
        self.z_sum(i, m.ring.at[i], m.czb.at[n], m.czm.at[n], m.ch.at[n])
        self.post(i, m.ch.at[n, 1 - self.x], m.cx.at[n], self.at_x)

    def c3(self, i, n):
        m = self.m
        self.arrived(i)
        m.cx[n] = m.cx[n] + m.ch[n, self.x]
        self.post(i, m.cx.at[n], m.cy.at[n], self.at_y)

    def c4(self, i, n):
        m = self.m
        self.arrived(i)
        m.cy[n] = m.cy[n] + m.cx[n]
        self.last(i, m.cy.at[n], m.fin.at[i, self.c])

    def keep(self, src, dst):
        copy = pltpu.make_async_copy(src, dst, self.m.fs.at[len(self.locals)])
        copy.start()
        self.locals.append(copy)

    def inner_gone(self):
        for j in range(4):
            self.swaps["inner%d" % j].wait_send()

    def send_dstore(self):
        m = self.m
        self.small_d = [
            self.send(m.dstore.at[device[0]], m.ds_in.at[i], m.dss.at[i], m.dsr.at[i], device) for i, device in enumerate(self.at_blk)
        ]

    def send_vec(self):
        m, vec = self.m, self.m.vec
        m.vsh[...] = jnp.zeros(m.vsh.shape, F32)
        for s in range(8):
            m.vsh[s, 0:13, 0:SHARD] = vec[0:13, s * SHARD : (s + 1) * SHARD]
            for part in range(4):
                begin = 4 * SHARD * s + SHARD * part
                row, col = 13 + begin // D, begin % D
                m.vsh[s, 13 + part : 14 + part, 0:SHARD] = vec[row : row + 1, col : col + SHARD]
        self.small_v = [
            self.send(m.vsh.at[device[0]], m.vin.at[i], m.vss.at[i], m.vsr.at[i], device) for i, device in enumerate(self.at_blk)
        ]

    def finish(self):
        for copies in self.cores.values():
            for copy in copies:
                copy.wait_recv()
        for name, copy in self.swaps.items():
            if name not in self.here:
                copy.wait_recv()
        gone = [self.swaps["inner%d" % j] for j in range(4)]
        for copy in self.sent:
            if not any(copy is other for other in gone):
                copy.wait_send()

        @pl.when(self.is_end)
        def _():
            for make in self.sent_end:
                make().wait_send()

        @pl.when(jnp.logical_not(self.is_end))
        def _():
            for make in self.sent_mid:
                make().wait_send()

        for copy in self.locals:
            copy.wait()

    def small_total(self):
        m = self.m
        for copy in self.small:
            copy.wait_recv()
        m.vec_out[...] = (m.vrep[0] + m.vrep[1]) + (m.vrep[2] + m.vrep[3])

    def small_sums(self):
        m = self.m
        total = m.dstore[self.b].astype(F32)
        for i, copy in enumerate(self.small_d):
            copy.wait_recv()
            total = total + m.ds_in[i].astype(F32)
        m.dstore_out[...] = total
        total = m.vsh[self.b]
        for i, copy in enumerate(self.small_v):
            copy.wait_recv()
            total = total + m.vin[i]
        m.vrep[self.r] = total
        self.small = [
            self.send(m.vrep.at[self.r], m.vrep.at[self.r], m.vps.at[i], m.vpr.at[i], device)
            for i, device in enumerate(self.at_rep)
        ]


SUM_OUT = ["result_out", "d_hidden", "fin", "dstore_out", "vec_out"]


def sum_kernel(names, *refs):
    m, at_col = Refs(names, refs), columns(True)
    layer(m, Net(m, at_col), at_col)


def run_sum(args):
    rows, own = args[0].shape[2], args[1].shape[1]
    slots = 8 * own
    n, half = len(PIECES), SHARD // 2
    na, nb, nc = (WAYS.count(way) for way in "ABC")
    table = layer_scratch(rows, slots, n)
    table.update(
        result=((rows, D), BF), xt=((R_ALL, rows), BF), xt_p=((R_ALL, rows), BF), act_t=((8, 2, 2 * SHARD, rows), BF),
        act_p=((8, 2 * SHARD, rows), BF), dmat=((rows, columns(True).end), BF), d_p=((rows, O_ALL), BF),
        dkv=((slots, 2 * D), BF), dkv_p=((slots, D), BF), dstore=((8, own, D), BF), vec=((24, D), F32),
        all_states=((8, own, D), BF), states_p=((8, own, D), BF),
        ax=((na, 4, 2, half, PART), BF), azb=((na, 3, 2, half, PART), BF), azm=((na, 2, half, PART), BF),
        ah=((na, 2, half, PART), BF), ay=((na, 2, half, PART), BF),
        by=((nb, 4, 2, half, PART), BF), bx=((nb, 4, half, PART), BF), bzb=((nb, 3, half, PART), BF),
        bzm=((nb, half, PART), BF), bh=((nb, half, PART), BF), bg=((nb, half, PART), BF),
        czb=((nc, 3, 2, 2, half, PART), BF), czm=((nc, 2, 2, half, PART), BF), ch=((nc, 2, 2, half, PART), BF),
        cx=((nc, 2, half, PART), BF), cy=((nc, 2, half, PART), BF), ds_in=((7, own, D), BF),
        vsh=((8, 24, 128), F32), vin=((7, 24, 128), F32), vrep=((4, 24, 128), F32),
    )
    sems = dict(
        w_sem=(13,), gs=(7,), gr=(7,), os=(24,), orr=(24,), ps=(n, 3), pr=(n, 3), zs=(n, 3), zr=(n, 4),
        cs=(n, 2), cr=(n, 2), fs=(2 * n + 2,), dss=(7,), dsr=(7,), vss=(7,), vsr=(7,), vps=(3,), vpr=(3,),
    )
    vmem, hbm, smem = (pl.BlockSpec(memory_space=s) for s in (pltpu.VMEM, pl.ANY, pltpu.SMEM))
    shape = jax.ShapeDtypeStruct
    return pl.pallas_call(
        functools.partial(sum_kernel, INPUTS + SUM_OUT + list(table) + list(sems)),
        out_shape=(
            shape((rows, D), BF), shape((rows, D), F32), shape((n, 2, 2, half, PART), BF), shape((own, D), F32), shape((24, 128), F32),
        ),
        in_specs=[vmem] * 4 + [smem] + [vmem] * 11 + [hbm] * 8,
        out_specs=(hbm, hbm, hbm, vmem, vmem),
        scratch_shapes=buffers(table) + [pltpu.SemaphoreType.DMA(dims) for dims in sems.values()],
        compiler_params=pltpu.CompilerParams(collective_id=0, has_side_effects=True, vmem_limit_bytes=VMEM_LIMIT),
        cost_estimate=pl.CostEstimate(flops=15 * 10**9, bytes_accessed=5 * 10**7, transcendentals=10**6),
    )(*small_inputs(args), *weight_inputs(args))


def place_kernel(result, d_hidden, fin, dstore, vec, *outs):
    (o_result, o_hidden, o_dstore, o_qkv, o_sbias, o_so, o_sob, o_n1, o_cq, o_cqb, o_ckv, o_cvb, o_co, o_cob, o_n2, o_fi, o_fib, o_fo, o_fob, o_n3) = outs
    o_result[...] = result[...]
    o_hidden[...] = d_hidden[...]
    o_dstore[...] = dstore[...]
    wide = {"qkv": o_qkv, "so": o_so, "cq": o_cq, "ckv": o_ckv, "co": o_co, "fi": o_fi}
    for i, (kind, part) in enumerate(PIECES):
        for c in range(2):
            values = fin[i, c].astype(F32)
            if kind == "fo":
                begin = c * 2 * SHARD + (part // 2) * SHARD
                o_fo[begin : begin + SHARD, (part % 2) * PART : (part % 2 + 1) * PART] = values
            else:
                ref = wide[kind]
                begin = part * D + c * PART
                ref[:, begin : begin + PART] = values
    for ref, row in ((o_sbias, 0), (o_n1, 3), (o_n2, 8), (o_n3, 11)):
        ref[...] = vec[row : row + 2, 0:SHARD]
    for ref, row in ((o_sob, 2), (o_cqb, 5), (o_cvb, 6), (o_cob, 7), (o_fob, 10)):
        ref[...] = vec[row, 0:SHARD]
    for part in range(4):
        o_fib[pl.ds(part * SHARD, SHARD)] = vec[13 + part, 0:SHARD]


def place(result, d_hidden, fin, dstore, vec):
    shape = lambda *dims: jax.ShapeDtypeStruct(dims, F32)
    return pl.pallas_call(
        place_kernel,
        out_shape=(
            jax.ShapeDtypeStruct(result.shape, BF), shape(*d_hidden.shape), shape(*dstore.shape), shape(SHARD, 3 * D), shape(2, SHARD), shape(SHARD, D), shape(SHARD), shape(2, SHARD),
            shape(SHARD, D), shape(SHARD), shape(SHARD, 2 * D), shape(SHARD), shape(SHARD, D), shape(SHARD), shape(2, SHARD),
            shape(SHARD, FF), shape(FF // 8), shape(FF // 8, D), shape(SHARD), shape(2, SHARD),
        ),
        compiler_params=pltpu.CompilerParams(vmem_limit_bytes=VMEM_LIMIT),
    )(result, d_hidden, fin.reshape(len(PIECES), 2, SHARD, PART), dstore, vec)


def sum_plainly(states, xt, act_t, dmat, dkv, dstore, vec):
    def total(value, dim):
        part = lax.psum_scatter(value, "blk", scatter_dimension=dim, tiled=True)
        return lax.psum(part.astype(BF), "rep").astype(F32)

    at_col = columns(False)

    def rows_of(start):
        return lax.slice_in_dim(xt, start, start + D, axis=0)

    def cols_of(start, width):
        return lax.slice_in_dim(dmat, start, start + width, axis=1)

    g_qkv = total(dot(rows_of(R_TOK), cols_of(at_col.proj, 3 * D)), 0)
    g_so = total(dot(rows_of(R_SMIX), cols_of(at_col.sb, D)), 0)
    g_cq = total(dot(rows_of(R_FIRST), cols_of(at_col.cq, D)), 0)
    g_co = total(dot(rows_of(R_CMIX), cols_of(at_col.cb, D)), 0)
    g_fi = total(dot(rows_of(R_SECOND), cols_of(at_col.inner, FF)), 0)
    g_fo = total(dot(act_t.reshape(FF, -1), cols_of(at_col.fb, D)), 0)
    g_ckv = total(dot_tn(states, dkv), 0)
    g_store = lax.psum_scatter(dstore.astype(F32), "blk", scatter_dimension=0, tiled=True)
    g_fib = total(vec[13:N_VEC].reshape(FF), 0)
    v = total(vec[:13].T, 0)
    two = lambda row: v[:, row : row + 2].T
    return (
        g_store, g_qkv, two(0), g_so, v[:, 2], two(3), g_cq, v[:, 5], g_ckv, v[:, 6], g_co, v[:, 7], two(8),
        g_fi, g_fib, g_fo, v[:, 10], two(11),
    )


def on_device(fast, *args):
    if fast:
        result, d_hidden, *grads = place(*run_sum(args))
    else:
        states_all = lax.all_gather(args[1][0], "blk", axis=0, tiled=True)
        result, d_hidden, *operands = run_plain(args, states_all)
        grads = sum_plainly(states_all, *operands)
    return (result[None, None], d_hidden[None, None], grads[0][None], *grads[1:])


def solution(mesh):
    fast = mesh.shape["blk"] == 8 and mesh.shape["rep"] == 4
    deep, flat = P("rep", "blk", None, None), P("rep", "blk", None)
    in_specs = (deep, flat, deep, deep, P("rep", "blk")) + (P(),) * 17 + (deep,)
    w, vec, two = P("blk", None), P("blk"), P(None, "blk")
    out_specs = (deep, deep, flat, w, two, w, vec, two, w, vec, w, vec, w, vec, two, w, vec, w, vec, two)
    return jax.shard_map(
        functools.partial(on_device, fast), mesh=mesh, in_specs=in_specs, out_specs=out_specs, check_vma=False
    )
```

```python
import functools
import typing

import jax
import jax.numpy as jnp
from jax import lax
from jax.experimental import pallas as pl
from jax.experimental.pallas import tpu as pltpu
from jax.sharding import PartitionSpec as P

D = 768
HEADS = 12
HD = 64
FF = 3072
EPS = 1e-05
NEG = -1e30
BF = jnp.bfloat16
F32 = jnp.float32
MESH = pl.DeviceIdType.MESH
VMEM_LIMIT = 63 * 2**20

N_VEC = 17
R_SECOND, R_TOK, R_SMIX, R_FIRST, R_CMIX, R_ALL = 0, 768, 1536, 2304, 3072, 3840
PART = 384
SHARD = D // 8
PRODUCTS = [("fo", i) for i in range(4)] + [("fi", i) for i in range(4)]
PRODUCTS += [("co", 0), ("cq", 0), ("ckv", 0), ("ckv", 1), ("so", 0), ("qkv", 0), ("qkv", 1), ("qkv", 2)]
LANES = 128
UNITS = PART // LANES
PIECES = [(i, 0, UNITS) for i in range(12)] + [(i, unit, 1) for i in range(12, 16) for unit in range(UNITS)]
WAYS = "BCAACABBBBABABBBCBAAABBB"
ORDER = (
    0, 1, 2, 3, 4, 5, 6, 101, 102, 100, 103, 7, 107, 106, 104, 8, 9, 10, 11, 105, 12, 13, 14, 15,
    16, 17, 18, 108, 19, 20, 21, 22, 110, 202, 200, 201, 122, 116, 203, 207, 111, 204, 205, 301, 23, 206, 109, 302,
    210, 120, 208, 113, 216, 304, 222, 123, 300, 402, 24, 303, 307, 114, 316, 401, 119, 211, 121, 305, 306, 403, 220, 115,
    112, 209, 310, 405, 308, 213, 400, 117, 404, 322, 223, 416, 407, 410, 502, 118, 219, 406, 500, 214, 320, 507, 501, 311,
    506, 408, 221, 212, 422, 420, 503, 319, 309, 215, 508, 313, 411, 522, 505, 419, 323, 312, 217, 218, 409, 511, 314, 504,
    413, 412, 516, 321, 423, 315, 510, 318, 317, 600, 509, 414, 607, 513, 421, 523, 606, 415, 520, 417, 418, 608, 622, 514,
    519, 521, 611, 515, 512, 517, 609, 613, 623, 518, 614, 621, 615, 617,
)
O_INNER, O_PROJ, O_SB, O_CQ, O_CB, O_FB, O_ALL = 0, 1536, 2688, 3072, 3456, 3840, 4608


class Columns(typing.NamedTuple):
    inner: int
    proj: int
    sb: int
    cq: int
    cb: int
    fb: int
    end: int


def columns(fast):
    return Columns(0, 0, 2304, 3072, 3840, 4608, 5376) if fast else Columns(0, 3072, 5376, 6144, 6912, 7680, 8448)


def dot(a, b):
    return lax.dot_general(a, b, (((1,), (0,)), ((), ())), preferred_element_type=F32)


def dot_nt(a, b):
    return lax.dot_general(a, b, (((1,), (1,)), ((), ())), preferred_element_type=F32)


def dot_tn(a, b):
    return lax.dot_general(a, b, (((0,), (0,)), ((), ())), preferred_element_type=F32)


def at(index, size):
    return pl.ds(pl.multiple_of(index * size, size), size)


def half_mask(half):
    lane = lax.broadcasted_iota(jnp.int32, (1, 2 * HD), 1)
    return ((lane >= HD) if half else (lane < HD)).astype(F32).astype(BF)


def total_row(values):
    return jnp.sum(values, axis=0, keepdims=True)


def gelu_and_slope(v):
    cdf = 0.5 * (1.0 + lax.erf(v * 0.7071067811865476))
    return v * cdf, cdf + v * (jnp.exp(-0.5 * v * v) * 0.3989422804014327)


def norm_rows(r):
    centered = r - jnp.mean(r, axis=-1, keepdims=True)
    rstd = lax.rsqrt(jnp.mean(centered * centered, axis=-1, keepdims=True) + EPS)
    return centered * rstd, rstd


def norm_rows_back(grad, xhat, rstd, gain):
    e = grad * gain
    mean_e = jnp.mean(e, axis=-1, keepdims=True)
    mean_x = jnp.mean(e * xhat, axis=-1, keepdims=True)
    return (e - mean_e - xhat * mean_x) * rstd


def attend(q_ref, k_ref, vt_ref, bias_ref, p_ref, mix_t_ref):
    scores = []
    for j in range(HEADS // 2):
        cols = slice(2 * HD * j, 2 * HD * (j + 1))
        q2, k2 = q_ref[:, cols], k_ref[:, cols]
        scores += [dot_nt(k2 * half_mask(half), q2) for half in range(2)]
    for h, st in enumerate(scores):
        st = st + bias_ref[...]
        e = jnp.exp(st - jnp.max(st, axis=0, keepdims=True))
        p_ref[h] = (e * (1.0 / jnp.sum(e, axis=0, keepdims=True))).astype(BF)
    for h in range(HEADS):
        rows = slice(HD * h, HD * (h + 1))
        mix_t_ref[rows, :] = dot(vt_ref[rows, :], p_ref[h]).astype(BF)


def attend_back(p_ref, dmix_ref, q_ref, v_ref, kt_ref, dq_t_ref, put, begin, end):
    parts = []
    for j in range(begin, end):
        cols = slice(2 * HD * j, 2 * HD * (j + 1))
        dm2, q2, v2 = dmix_ref[:, cols], q_ref[:, cols], v_ref[:, cols]
        parts += [(2 * j + half, dm2 * half_mask(half), q2 * half_mask(half), dot_nt(v2 * half_mask(half), dm2)) for half in range(2)]
    grads = []
    for h, dm, q, dp in parts:
        p = p_ref[h].astype(F32)
        t = p * dp
        grads.append((t - p * jnp.sum(t, axis=0, keepdims=True)).astype(BF))
    for n, (h, dm, q, dp) in enumerate(parts):
        dq_t_ref[HD * h : HD * (h + 1), :] = dot(kt_ref[HD * h : HD * (h + 1), :], grads[n]).astype(BF)
    for n in range(0, len(parts), 2):
        (h, dm0, q0, _), (_, dm1, q1, _) = parts[n : n + 2]
        put(h // 2, dot(grads[n], q0) + dot(grads[n + 1], q1), dot(p_ref[h], dm0) + dot(p_ref[h + 1], dm1))


class Refs:
    def __init__(self, names, refs):
        for name, ref in zip(names, refs, strict=True):
            setattr(self, name, ref)


class Inputs(typing.NamedTuple):
    tokens: typing.Any
    states: typing.Any
    retrieved: typing.Any
    live: typing.Any
    lengths: typing.Any
    self_bias: typing.Any
    self_out_bias: typing.Any
    norm1: typing.Any
    cq_bias: typing.Any
    cv_bias: typing.Any
    co_bias: typing.Any
    norm2: typing.Any
    fi_bias: typing.Any
    fo_bias: typing.Any
    norm3: typing.Any
    cotangent: typing.Any
    h_qkv: typing.Any
    h_qkv6: typing.Any
    h_so: typing.Any
    h_cq: typing.Any
    h_ckv: typing.Any
    h_co: typing.Any
    h_fi: typing.Any
    h_fo: typing.Any


INPUTS = list(Inputs._fields)


def layer(m, net, at_col):
    rows = m.tokens.shape[0]
    length = m.lengths[0, 0]
    scale = HD**-0.5
    xt, dmat, vec = m.xt, m.dmat, m.vec
    copies = {}
    order = [("so", m.h_so, m.w_so), ("cq", m.h_cq, m.w_cq), ("ckv", m.h_ckv, m.w_ckv), ("co", m.h_co, m.w_co), ("fi", m.h_fi, m.w_fi)]

    def fetch_units(src, first, count, sem):
        for i in range(count):
            pltpu.make_async_copy(src(i), m.ring.at[first + i], sem).start()

    def have_units(first, count, sem):
        here = m.ring.at[first : first + count]
        pltpu.make_async_copy(here, here, sem).wait()

    def weight(slot):
        return jnp.concatenate([m.ring[UNITS * slot + unit].reshape(D, LANES) for unit in range(UNITS)], axis=1)

    fetch_units(lambda i: m.h_qkv6.at[:, :, :, :, i * LANES : (i + 1) * LANES], 0, 18, m.w_sem.at[6])
    for i, (name, src, dst) in enumerate(order):
        copies[name] = pltpu.make_async_copy(src, dst, m.w_sem.at[i])
        copies[name].start()
    fetch_units(lambda i: m.h_fo.at[i // 6, :, :, :, :, i % 6 * LANES : (i % 6 + 1) * LANES], 24, 24, m.w_sem.at[7])
    if net:
        net.greet()

    def piece(name):
        return slice(getattr(at_col, name), getattr(at_col, name) + D)

    xt[R_TOK : R_TOK + D, :] = m.tokens[...].T
    key_at = lax.broadcasted_iota(jnp.int32, (rows, rows), 0)
    query_at = lax.broadcasted_iota(jnp.int32, (rows, rows), 1)
    m.bias_s[...] = jnp.where((key_at <= query_at) & (key_at < length), 0.0, NEG)
    if net:
        net.begin()
    topk = m.retrieved.shape[0]
    slots = m.bias_c.shape[0]
    slot_rank = lax.broadcasted_iota(jnp.int32, (topk, rows), 0)
    chosen = jnp.where((m.live[...] > 0) | (slot_rank == 0), m.retrieved[...], -1)

    def mask_rows(i, _):
        ids = lax.broadcasted_iota(jnp.int32, (32, rows), 0) + i * 32
        hit = jnp.zeros((32, rows), jnp.bool_)
        for j in range(topk):
            hit = hit | (ids == chosen[j : j + 1, :])
        m.bias_c[at(i, 32), :] = jnp.where(hit, 0.0, NEG)
        return 0

    lax.fori_loop(0, slots // 32, mask_rows, 0)

    for i, (ref, bias) in enumerate(((m.q, 0), (m.q, 0), (m.k, None), (m.k, None), (m.v, 1), (m.v, 1))):
        if i == 0:
            have_units(0, 18, m.w_sem.at[6])
        cols = slice((i % 2) * PART, (i % 2 + 1) * PART)
        got = dot(m.tokens[...], weight(i))
        if bias is not None:
            got = got + m.self_bias[bias : bias + 1, cols]
        got = got.astype(BF)
        ref[:, cols] = got * scale if bias == 0 else got
    m.vt[...] = m.v[...].T
    attend(m.q, m.k, m.vt, m.bias_s, m.p_s, xt.at[R_SMIX : R_SMIX + D])
    m.vt[...] = m.k[...].T * scale
    copies["so"].wait()
    if net:
        net.swap_rows("smix")
    m.mix_b[...] = xt[R_SMIX : R_SMIX + D, :].T
    m.acc[...] = dot(m.mix_b[...], m.w_so[...])

    def ln1(rs):
        xhat, rstd = norm_rows(m.tokens[rs, :].astype(F32) + m.acc[rs, :] + m.self_out_bias[...][None, :])
        m.xhat1[rs, :] = xhat
        m.rstd1[rs, :] = rstd
        m.sec_b[rs, :] = (xhat * m.norm1[0:1, :] + m.norm1[1:2, :]).astype(BF)

    ln1(slice(0, rows))
    xt[R_FIRST : R_FIRST + D, :] = m.sec_b[...].T
    if net:
        net.swap_rows("first")

    copies["cq"].wait()
    m.k[...] = (dot(m.sec_b[...], m.w_cq[...]) + m.cq_bias[...][None, :]).astype(BF) * scale
    copies["ckv"].wait()
    if net:
        net.have_states()
    states = m.all_states[...].reshape(slots, D)
    m.sk[...] = dot(states, m.w_ckv[:, :D]).astype(BF)
    m.sv[...] = (dot(states, m.w_ckv[:, D:]) + m.cv_bias[...][None, :]).astype(BF)
    m.svt[...] = m.sv[...].T
    attend(m.k, m.sk, m.svt, m.bias_c, m.p_c, xt.at[R_CMIX : R_CMIX + D])
    m.svt[...] = m.sk[...].T * scale
    copies["co"].wait()
    if net:
        net.swap_rows("cmix")
    m.mix_b[...] = xt[R_CMIX : R_CMIX + D, :].T
    m.acc[...] = dot(m.mix_b[...], m.w_co[...])

    def ln2(rs):
        first = m.xhat1[rs, :] * m.norm1[0:1, :] + m.norm1[1:2, :]
        xhat, rstd = norm_rows(first + m.acc[rs, :] + m.co_bias[...][None, :])
        m.xhat2[rs, :] = xhat
        m.rstd2[rs, :] = rstd
        m.sec_b[rs, :] = (xhat * m.norm2[0:1, :] + m.norm2[1:2, :]).astype(BF)

    ln2(slice(0, rows))
    xt[R_SECOND : R_SECOND + D, :] = m.sec_b[...].T
    if net:
        net.swap_rows("second")

    copies["fi"].wait()
    have_units(24, 24, m.w_sem.at[7])
    for j in range(FF // D):
        cols = slice(j * D, (j + 1) * D)
        m.acc2[...] = dot(m.sec_b[...], m.w_fi[:, cols])
        bias = m.fi_bias[cols][None, :]

        def gelu(rs):
            a, s = gelu_and_slope(m.acc2[rs, :] + bias)
            m.mix_b[rs, :] = a.astype(BF)
            m.slope[rs, cols] = s.astype(BF)

        gelu(slice(0, rows))
        m.act_t[2 * j : 2 * j + 2] = m.mix_b[...].T.reshape(2, 2, 2 * SHARD, rows)
        if net:
            net.swap_act(j)
        for part in range(2):
            got = dot(m.mix_b[...], weight(8 + 2 * j + part))
            here = slice(part * PART, (part + 1) * PART)
            m.acc[:, here] = got if j == 0 else m.acc[:, here] + got

    def ln3(rs):
        second = m.xhat2[rs, :] * m.norm2[0:1, :] + m.norm2[1:2, :]
        xhat, rstd = norm_rows(second + m.acc[rs, :] + m.fo_bias[...][None, :])
        m.result[rs, :] = (xhat * m.norm3[0:1, :] + m.norm3[1:2, :]).astype(BF)
        place = lax.broadcasted_iota(jnp.int32, (rows, 1), 0)
        g = m.cotangent[rs, :].astype(F32) * jnp.where(place < length, 1.0, 0.0)
        d = norm_rows_back(g, xhat, rstd, m.norm3[0:1, :])
        m.d_res[rs, :] = d
        db = d.astype(BF)
        dmat[rs, piece("fb")] = db
        return total_row(g * xhat), total_row(g), total_row(db.astype(F32))

    vec[N_VEC:, :] = jnp.zeros((vec.shape[0] - N_VEC, D), F32)
    vec[11:12, :], vec[12:13, :], vec[10:11, :] = ln3(slice(0, rows))
    if net:
        net.swap("fb")

    steps = []

    def feed_back(j):
        cols = slice(j * D, (j + 1) * D)
        inner = slice(at_col.inner + j * D, at_col.inner + (j + 1) * D)
        left, right = (dmat[:, at_col.fb + part * PART : at_col.fb + (part + 1) * PART] for part in range(2))
        m.acc2[...] = dot_nt(left, weight(8 + 2 * j)) + dot_nt(right, weight(9 + 2 * j))

        def inner_rows(rs):
            d = (m.slope[rs, cols].astype(F32) * m.acc2[rs, :]).astype(BF)
            dmat[rs, inner] = d
            return total_row(d.astype(F32))

        vec[13 + j : 14 + j, :] = inner_rows(slice(0, rows))
        if net:
            net.swap("inner", j)

    def feed_back_x(j):
        inner = slice(at_col.inner + j * D, at_col.inner + (j + 1) * D)
        got = dot_nt(dmat[:, inner], m.w_fi[:, j * D : (j + 1) * D])
        m.acc[...] = (m.d_res[...] if j == 0 else m.acc[...]) + got

    for j in range(FF // D):
        steps += [functools.partial(feed_back, j), functools.partial(feed_back_x, j)]

    def norm_back(xhat_ref, rstd_ref, norm, name):
        def block(rs):
            g, xhat = m.acc[rs, :], xhat_ref[rs, :]
            d = norm_rows_back(g, xhat, rstd_ref[rs, :], norm[0:1, :])
            m.d_res[rs, :] = d
            db = d.astype(BF)
            dmat[rs, piece(name)] = db
            return total_row(g * xhat), total_row(g), total_row(db.astype(F32))

        sums = block(slice(0, rows))
        if net:
            net.swap(name)
        return sums

    def back_norm2():
        copies["qkv"] = pltpu.make_async_copy(m.h_qkv, m.w_fi.at[:, 0 : 3 * D], m.w_sem.at[5])
        copies["qkv"].start()
        vec[8:9, :], vec[9:10, :], vec[7:8, :] = norm_back(m.xhat2, m.rstd2, m.norm2, "cb")

    def back_cross_out():
        m.mix_b[...] = dot_nt(dmat[:, piece("cb")], m.w_co[...]).astype(BF)

    def put_store(j, dk, dv):
        cols = slice(2 * HD * j, 2 * HD * (j + 1))
        m.dkv[:, cols] = dk.astype(BF)
        m.dkv[:, D + 2 * HD * j : D + 2 * HD * (j + 1)] = dv.astype(BF)
        vec[6:7, cols] = total_row(dv)

    def back_cross(part):
        attend_back(m.p_c, m.mix_b, m.k, m.sv, m.svt, m.dqt, put_store, 2 * part, 2 * part + 2)
        if net and part == 2:
            net.swap("dkv", 0)
            net.swap("dkv", 1)

    def back_query():
        dq = m.dqt[...].T
        dmat[:, piece("cq")] = dq
        if net:
            net.swap("cq")
        vec[5:6, :] = total_row(dq.astype(F32))

    def back_store():
        m.dstore[...] = dot_nt(m.dkv[...], m.w_ckv[...]).astype(BF).reshape(m.dstore.shape)
        if net:
            net.send_dstore()

    def back_first():
        m.acc[...] = m.d_res[...] + dot_nt(dmat[:, piece("cq")], m.w_cq[...])

    def back_norm1():
        if net:
            net.inner_gone()
        vec[3:4, :], vec[4:5, :], vec[2:3, :] = norm_back(m.xhat1, m.rstd1, m.norm1, "sb")

    def back_self_out():
        m.mix_b[...] = dot_nt(dmat[:, piece("sb")], m.w_so[...]).astype(BF)

    def put_self(j, dk, dv):
        dvb = dv.astype(BF)
        begin = at_col.proj + D + 2 * HD * j
        dmat[:, begin : begin + 2 * HD] = dk.astype(BF)
        dmat[:, begin + D : begin + D + 2 * HD] = dvb
        vec[1:2, 2 * HD * j : 2 * HD * (j + 1)] = total_row(dvb.astype(F32))

    def back_self(part):
        attend_back(m.p_s, m.mix_b, m.q, m.v, m.vt, m.dqt, put_self, 2 * part, 2 * part + 2)
        if net and part == 2:
            net.swap("proj", 1)
            net.swap("proj", 2)

    def back_proj():
        dq = m.dqt[...].T
        dmat[:, at_col.proj : at_col.proj + D] = dq
        if net:
            net.swap("proj", 0)
        vec[0:1, :] = total_row(dq.astype(F32))
        if net:
            net.send_vec()

    def back_hidden():
        copies["qkv"].wait()
        m.acc[...] = m.d_res[...] + dot_nt(dmat[:, at_col.proj : at_col.proj + 3 * D], m.w_fi[:, 0 : 3 * D])
        if net:
            net.keep(m.acc, m.d_hidden, m.fs.at[1])
            net.keep(m.result, m.result_out, m.fs.at[2])

    steps += [back_norm2, back_cross_out] + [functools.partial(back_cross, part) for part in range(3)]
    steps += [back_query, back_store, back_first, back_norm1, back_self_out] + [functools.partial(back_self, part) for part in range(3)]
    steps += [back_proj, back_hidden]
    if net:
        steps += [net.small_sums, net.small_total]
        steps += [functools.partial(net.make, i) for i in range(len(PRODUCTS))]
        for number in ORDER:
            if number < 100:
                steps[number]()
            else:
                net.step(number // 100 - 1, number % 100)
        net.finish()
    else:
        for step in steps:
            step()


def weight_inputs(args):
    self_qkv, self_out, cross_q, cross_kv, cross_out, ffn_in, ffn_out = (args[i] for i in (5, 7, 10, 12, 14, 17, 19))
    return (self_qkv, self_qkv.reshape(4, 2, 2, D // 16, 3 * D), self_out, cross_q, cross_kv, cross_out, ffn_in,
            ffn_out.reshape(FF // D, 4, 2, 2, D // 16, D))


def small_inputs(args):
    (hidden, store, retrieved, live, lengths, _, self_bias, _, self_out_bias, norm1, _, cross_q_bias,
     _, cross_v_bias, _, cross_out_bias, norm2, _, ffn_in_bias, _, ffn_out_bias, norm3, cotangent) = args
    return (
        hidden[0, 0], store[0], jnp.swapaxes(retrieved[0, 0], 0, 1), jnp.swapaxes(live[0, 0], 0, 1), lengths, self_bias,
        self_out_bias, norm1, cross_q_bias, cross_v_bias, cross_out_bias, norm2, ffn_in_bias, ffn_out_bias, norm3, cotangent[0, 0],
    )


def layer_scratch(rows, slots):
    wide = (rows, D)
    return dict(
        ring=((UNITS * 16, 4, 2, 2, D // 16, LANES), BF), w_so=((D, D), BF), w_cq=((D, D), BF), w_ckv=((D, 2 * D), BF),
        w_co=((D, D), BF), w_fi=((D, FF), BF),
        q=(wide, BF), k=(wide, BF), v=(wide, BF), vt=((D, rows), BF), bias_s=((rows, rows), F32),
        p_s=((HEADS, rows, rows), BF), sk=((slots, D), BF), sv=((slots, D), BF), svt=((D, slots), BF),
        bias_c=((slots, rows), F32), p_c=((HEADS, slots, rows), BF), mix_b=(wide, BF),
        acc=(wide, F32), acc2=(wide, F32), xhat1=(wide, F32), xhat2=(wide, F32),
        sec_b=(wide, BF), slope=((rows, FF), BF), d_res=(wide, F32), dqt=((D, rows), BF),
        rstd1=((rows, 1), F32), rstd2=((rows, 1), F32),
    )


def buffers(table):
    return [pltpu.VMEM(dims, kind) for dims, kind in table.values()]


PLAIN_OUT = ["result", "acc", "xt", "act_t", "dmat", "dkv", "dstore", "vec"]


def plain_kernel(names, *refs):
    layer(Refs(names, refs), None, columns(False))


def run_plain(args, states_all):
    rows, slots = args[0].shape[2], states_all.shape[0]
    at_col = columns(False)
    table = layer_scratch(rows, slots)
    del table["acc"]
    vmem, hbm, smem = (pl.BlockSpec(memory_space=s) for s in (pltpu.VMEM, pl.ANY, pltpu.SMEM))
    shape = jax.ShapeDtypeStruct
    names = INPUTS + PLAIN_OUT + list(table) + ["w_sem"]
    names[names.index("states")] = "all_states"
    small = small_inputs(args)
    outs = pl.pallas_call(
        functools.partial(plain_kernel, names),
        out_shape=(
            shape((rows, D), BF), shape((rows, D), F32), shape((R_ALL, rows), BF), shape((8, 2, 2 * SHARD, rows), BF),
            shape((rows, at_col.end), BF), shape((slots, 2 * D), BF), shape((slots, D), BF), shape((24, D), F32),
        ),
        in_specs=[vmem] * 4 + [smem] + [vmem] * 11 + [hbm] * 8,
        out_specs=(vmem,) * 8,
        scratch_shapes=buffers(table) + [pltpu.SemaphoreType.DMA((8,))],
        compiler_params=pltpu.CompilerParams(vmem_limit_bytes=VMEM_LIMIT),
    )(small[0], states_all, *small[2:], *weight_inputs(args))
    return outs


class Net:
    def __init__(self, m, at_col):
        self.m, self.at_col = m, at_col
        b, r = lax.axis_index("blk"), lax.axis_index("rep")
        self.b, self.r = b, r
        self.z, self.x, self.y, self.c = b // 2, b % 2, r // 2, r % 2
        z, x, y, c = self.z, self.x, self.y, self.c
        self.at_x = (z * 2 + 1 - x, r)
        self.at_y = (b, (1 - y) * 2 + c)
        self.at_c = (b, y * 2 + 1 - c)
        side = z // 2
        self.side, self.is_end = side, jnp.logical_or(z == 0, z == 3)
        self.at_mid, self.at_end = ((1 + side) * 2 + x, r), (3 * side * 2 + x, r)
        self.at_near, self.at_far = ((2 - side) * 2 + x, r), (3 * (1 - side) * 2 + x, r)
        self.at_blk = [(lax.rem(b + step, 8), r) for step in range(1, 8)]
        self.at_rep = [(b, lax.rem(r + step, 4)) for step in range(1, 4)]
        self.here, self.swapped = [], []
        self.steps, self.chain = {}, []
        self.span, self.own, taken = [], [], dict.fromkeys(WAYS, 0)
        for way, (product, unit, units) in zip(WAYS, PIECES, strict=True):
            self.span.append(slice(taken[way], taken[way] + units))
            self.own.append(slice(UNITS * product + unit, UNITS * product + unit + units))
            taken[way] += units
        self.made = []

    def copy(self, src, dst, s_sem, r_sem, device):
        return pltpu.make_async_remote_copy(
            src_ref=src, dst_ref=dst, send_sem=s_sem, recv_sem=r_sem, device_id=device, device_id_type=MESH
        )

    def send(self, *args):
        copy = self.copy(*args)
        copy.start()
        return copy

    def sized(self, ref, s_sem, r_sem):
        return self.copy(ref, ref, s_sem, r_sem, self.at_c)

    def greet(self):
        barrier = pltpu.get_barrier_semaphore()
        for device in self.at_blk + self.at_rep:
            pl.semaphore_signal(barrier, inc=1, device_id=device, device_id_type=MESH)

    def begin(self):
        m = self.m
        m.all_states[self.b] = m.states[...]
        pl.semaphore_wait(pltpu.get_barrier_semaphore(), len(self.at_blk) + len(self.at_rep))
        for device in self.at_blk:
            self.send(m.states, m.all_states.at[self.b], m.ss.at[0], m.sr.at[0], device)
        self.swap_rows("tok")

    def have_states(self):
        m = self.m
        self.sized(m.all_states.at[0:7], m.ss.at[0], m.sr.at[0]).wait_recv()
        self.trade("states", m.all_states, m.states_p)

    def group(self, name):
        m = self.m
        part = lambda start, width: m.d_p.at[:, start : start + width]
        table = {
            "rows": m.xt_p, "act": m.act_p, "fb": part(O_FB, D), "inner": part(O_INNER, 4 * PART), "cb": part(O_CB, PART),
            "cq": part(O_CQ, PART), "dkv": m.dkv_p, "sb": part(O_SB, PART), "proj": part(O_PROJ, 3 * PART), "states": m.states_p,
        }
        i = list(table).index(name)
        return table[name], m.os.at[i], m.orr.at[i]

    def trade(self, name, src, dst):
        _, s_sem, r_sem = self.group(name)
        self.send(src, dst, s_sem, r_sem, self.at_c)
        if name not in self.swapped:
            self.swapped.append(name)

    def need(self, *names):
        for name in names:
            if name not in self.here:
                self.sized(*self.group(name)).wait_recv()
                self.here.append(name)

    def swap_rows(self, name):
        row = {"tok": R_TOK, "smix": R_SMIX, "first": R_FIRST, "cmix": R_CMIX, "second": R_SECOND}[name]
        self.trade("rows", self.m.xt.at[row : row + D], self.m.xt_p.at[row : row + D])

    def swap_act(self, j):
        here = slice(2 * j, 2 * j + 2)
        self.trade("act", self.m.act_t.at[here, 1 - self.c], self.m.act_p.at[here])

    def half(self, start, who):
        return pl.ds(pl.multiple_of(start + who * PART, 128), PART)

    def operand(self, name, part):
        m, at_col = self.m, self.at_col
        if name == "dkv":
            return m.dkv, part * D, m.dkv_p, part * PART
        place = {"inner": O_INNER, "proj": O_PROJ, "sb": O_SB, "cq": O_CQ, "cb": O_CB}[name]
        return m.dmat, getattr(at_col, name) + part * D, m.d_p, place + part * PART

    def swap(self, name, part=0):
        m = self.m
        if name == "fb":
            start = self.at_col.fb
            self.trade("fb", m.dmat.at[:, start : start + D], m.d_p.at[:, O_FB : O_FB + D])
            return
        ref, start, there, place = self.operand(name, part)
        self.trade(name, ref.at[:, self.half(start, 1 - self.c)], there.at[:, place : place + PART])

    def product(self, i):
        m = self.m
        kind, part = PRODUCTS[i]
        if kind == "fo":
            self.need("fb", "act")
            up = slice((part // 2) * SHARD, (part // 2 + 1) * SHARD)
            left = m.act_t[:, self.c, up, :].reshape(D, -1)
            left_p = m.act_p[:, up, :].reshape(D, -1)
            begin = (part % 2) * PART
            right = m.dmat[:, self.at_col.fb + begin : self.at_col.fb + begin + PART]
            right_p = m.d_p[:, O_FB + begin : O_FB + begin + PART]
        else:
            name, row = {"fi": ("inner", R_SECOND), "co": ("cb", R_CMIX), "cq": ("cq", R_FIRST), "ckv": ("dkv", 0),
                         "so": ("sb", R_SMIX), "qkv": ("proj", R_TOK)}[kind]
            self.need(name, "states" if kind == "ckv" else "rows")
            ref, start, there, place = self.operand(name, part)
            right = ref[:, self.half(start, self.c)]
            right_p = there[:, place : place + PART]
            if kind == "ckv":
                left = m.all_states[...].reshape(-1, D).T
                left_p = m.states_p[...].reshape(-1, D).T
            else:
                left, left_p = m.xt[row : row + D, :], m.xt_p[row : row + D, :]
        total = (dot(left, right) + dot(left_p, right_p)).astype(BF)
        for unit in range(UNITS):
            m.ring[UNITS * i + unit] = total[:, unit * LANES : (unit + 1) * LANES].reshape(4, 2, 2, SHARD // 2, LANES)

    def make(self, i):
        if i not in self.made:
            self.made.append(i)
            self.product(i)

    def step(self, stage, i):
        if stage == 0:
            self.make(PIECES[i][0])
        ways = {
            "A": (self.a0, self.a1, self.a2, self.a3, self.a4),
            "B": (self.b0, self.b1, self.b2, self.b3, self.b4, self.b5),
            "C": (self.c0, self.c1, self.c2, self.c3, self.c4),
        }
        ways[WAYS[i]][stage](i, self.span[i], self.own[i])

    def post(self, i, src, dst, device):
        sent = self.steps.setdefault(i, [])
        if sent:
            sent[-1].wait_send()
        sent.append(self.send(src, dst, self.m.ps.at[i], self.m.pr.at[i, len(sent)], device))

    def arrived(self, i):
        self.steps[i][-1].wait_recv()

    def z_send(self, i, part, zb):
        m, others, edge = self.m, pl.ds(1 - self.side, 3), 3 * self.side

        @pl.when(self.is_end)
        def _():
            self.send(part.at[:, others], zb, m.zs.at[i], m.zr.at[i, 0], self.at_mid)

        @pl.when(jnp.logical_not(self.is_end))
        def _():
            self.send(part.at[:, edge], zb.at[:, 0], m.zs.at[i], m.zr.at[i, 0], self.at_end)

    def z_pass(self, i, part, zb, zm):
        m, side = self.m, self.side
        far, near = 2 * (1 - side), 1

        @pl.when(jnp.logical_not(self.is_end))
        def _():
            self.sized(zb, m.zs.at[i], m.zr.at[i, 0]).wait_recv()
            zb[:, far] = zb[:, far] + part[:, 3 * (1 - side)]
            self.send(zb.at[:, far], zb.at[:, 1], m.zs.at[i], m.zr.at[i, 1], self.at_far)
            zb[:, near] = zb[:, near] + part[:, 2 - side]
            self.send(zb.at[:, near], zm, m.zs.at[i], m.zr.at[i, 1], self.at_near)

    def z_sum(self, i, part, zb, zm, out):
        m, side = self.m, self.side

        @pl.when(self.is_end)
        def _():
            self.sized(zm, m.zs.at[i], m.zr.at[i, 0]).wait_recv()
            self.sized(zm, m.zs.at[i], m.zr.at[i, 1]).wait_recv()
            out[...] = (part[:, self.z].astype(F32) + zb[:, 0].astype(F32) + zb[:, 1].astype(F32)).astype(BF)

        @pl.when(jnp.logical_not(self.is_end))
        def _():
            self.sized(zm, m.zs.at[i], m.zr.at[i, 1]).wait_recv()
            out[...] = (part[:, self.z].astype(F32) + zb[:, 2 * side].astype(F32) + zm[...].astype(F32)).astype(BF)

        self.chain.append((zb, i))

    def last(self, ref, there):
        m = self.m
        pltpu.make_async_copy(ref, there, m.fs.at[0]).start()
        self.send(ref, there, m.cs.at[0], m.cr.at[0], self.at_c)

    def a0(self, i, at, own):
        self.post(i, self.m.ring.at[own, :, 1 - self.x], self.m.ax.at[at], self.at_x)

    def a1(self, i, at, own):
        m = self.m
        self.arrived(i)
        m.ax[at] = m.ax[at] + m.ring[own, :, self.x]
        self.z_send(i, m.ax.at[at], m.azb.at[at])

    def a2(self, i, at, own):
        self.z_pass(i, self.m.ax.at[at], self.m.azb.at[at], self.m.azm.at[at])

    def a3(self, i, at, own):
        m = self.m
        self.z_sum(i, m.ax.at[at], m.azb.at[at], m.azm.at[at], m.ah.at[at])
        self.post(i, m.ah.at[at], m.ay.at[at], self.at_y)

    def a4(self, i, at, own):
        m = self.m
        self.arrived(i)
        m.ay[at] = m.ay[at] + m.ah[at]
        self.last(m.ay.at[at], m.fin.at[own, self.c])

    def b0(self, i, at, own):
        self.post(i, self.m.ring.at[own, :, :, 1 - self.y], self.m.by.at[at], self.at_y)

    def b1(self, i, at, own):
        m = self.m
        self.arrived(i)
        m.by[at] = m.by[at] + m.ring[own, :, :, self.y]
        self.post(i, m.by.at[at, :, 1 - self.x], m.bx.at[at], self.at_x)

    def b2(self, i, at, own):
        m = self.m
        self.arrived(i)
        m.bx[at] = m.bx[at] + m.by[at, :, self.x]
        self.z_send(i, m.bx.at[at], m.bzb.at[at])

    def b3(self, i, at, own):
        self.z_pass(i, self.m.bx.at[at], self.m.bzb.at[at], self.m.bzm.at[at])

    def b4(self, i, at, own):
        m = self.m
        self.z_sum(i, m.bx.at[at], m.bzb.at[at], m.bzm.at[at], m.bh.at[at])
        self.post(i, m.bh.at[at], m.bg.at[at], self.at_y)
        self.last(m.bh.at[at], m.fin.at[own, self.c, self.y])

    def b5(self, i, at, own):
        self.arrived(i)
        self.last(self.m.bg.at[at], self.m.fin.at[own, self.c, 1 - self.y])

    def c0(self, i, at, own):
        self.z_send(i, self.m.ring.at[own], self.m.czb.at[at])

    def c1(self, i, at, own):
        self.z_pass(i, self.m.ring.at[own], self.m.czb.at[at], self.m.czm.at[at])

    def c2(self, i, at, own):
        m = self.m
        self.z_sum(i, m.ring.at[own], m.czb.at[at], m.czm.at[at], m.ch.at[at])
        self.post(i, m.ch.at[at, 1 - self.x], m.cx.at[at], self.at_x)

    def c3(self, i, at, own):
        m = self.m
        self.arrived(i)
        m.cx[at] = m.cx[at] + m.ch[at, self.x]
        self.post(i, m.cx.at[at], m.cy.at[at], self.at_y)

    def c4(self, i, at, own):
        m = self.m
        self.arrived(i)
        m.cy[at] = m.cy[at] + m.cx[at]
        self.last(m.cy.at[at], m.fin.at[own, self.c])

    def keep(self, src, dst, sem):
        pltpu.make_async_copy(src, dst, sem).start()

    def inner_gone(self):
        self.sized(*self.group("inner")).wait_send()

    def send_dstore(self):
        m = self.m
        for i, device in enumerate(self.at_blk):
            self.send(m.dstore.at[device[0]], m.ds_in.at[i], m.ss.at[1], m.sr.at[1], device)

    def send_vec(self):
        m, vec = self.m, self.m.vec
        m.vsh[...] = jnp.zeros(m.vsh.shape, F32)
        for s in range(8):
            m.vsh[s, 0:13, 0:SHARD] = vec[0:13, s * SHARD : (s + 1) * SHARD]
            for part in range(4):
                begin = 4 * SHARD * s + SHARD * part
                row, col = 13 + begin // D, begin % D
                m.vsh[s, 13 + part : 14 + part, 0:SHARD] = vec[row : row + 1, col : col + SHARD]
        for i, device in enumerate(self.at_blk):
            self.send(m.vsh.at[device[0]], m.vin.at[i], m.ss.at[2], m.sr.at[2], device)

    def finish(self):
        m = self.m
        for name in self.swapped:
            self.need(name)
            if name != "inner":
                self.sized(*self.group(name)).wait_send()
        for sent in self.steps.values():
            sent[-1].wait_send()
        for zb, i in self.chain:
            self.sized(zb, m.zs.at[i], m.zr.at[i, 0]).wait_send()
        for k, ref in enumerate((m.all_states.at[0:7], m.ds_in, m.vin, m.vrep.at[0:3])):
            self.sized(ref, m.ss.at[k], m.sr.at[k]).wait_send()
        half = m.fin.at[:, self.c]
        self.sized(half, m.cs.at[0], m.cr.at[0]).wait()
        pltpu.make_async_copy(half, half, m.fs.at[0]).wait()
        pltpu.make_async_copy(m.acc, m.d_hidden, m.fs.at[1]).wait()
        pltpu.make_async_copy(m.result, m.result_out, m.fs.at[2]).wait()

    def small_total(self):
        m = self.m
        self.sized(m.vrep.at[0:3], m.ss.at[3], m.sr.at[3]).wait_recv()
        m.vec_out[...] = (m.vrep[0] + m.vrep[1]) + (m.vrep[2] + m.vrep[3])

    def small_sums(self):
        m = self.m
        self.sized(m.ds_in, m.ss.at[1], m.sr.at[1]).wait_recv()
        total = m.dstore[self.b].astype(F32)
        for i in range(7):
            total = total + m.ds_in[i].astype(F32)
        m.dstore_out[...] = total
        self.sized(m.vin, m.ss.at[2], m.sr.at[2]).wait_recv()
        total = m.vsh[self.b]
        for i in range(7):
            total = total + m.vin[i]
        m.vrep[self.r] = total
        for device in self.at_rep:
            self.send(m.vrep.at[self.r], m.vrep.at[self.r], m.ss.at[3], m.sr.at[3], device)


SUM_OUT = ["result_out", "d_hidden", "fin", "dstore_out", "vec_out"]


def sum_kernel(names, *refs):
    m, at_col = Refs(names, refs), columns(True)
    layer(m, Net(m, at_col), at_col)


def run_sum(args):
    rows, own = args[0].shape[2], args[1].shape[1]
    slots = 8 * own
    n, half = len(PIECES), SHARD // 2
    na, nb, nc = (sum(piece[2] for piece, its in zip(PIECES, WAYS, strict=True) if its == way) for way in "ABC")
    table = layer_scratch(rows, slots)
    table.update(
        result=((rows, D), BF), xt=((R_ALL, rows), BF), xt_p=((R_ALL, rows), BF), act_t=((8, 2, 2 * SHARD, rows), BF),
        act_p=((8, 2 * SHARD, rows), BF), dmat=((rows, columns(True).end), BF), d_p=((rows, O_ALL), BF),
        dkv=((slots, 2 * D), BF), dkv_p=((slots, D), BF), dstore=((8, own, D), BF), vec=((24, D), F32),
        all_states=((8, own, D), BF), states_p=((8, own, D), BF),
        ax=((na, 4, 2, half, LANES), BF), azb=((na, 3, 2, half, LANES), BF), azm=((na, 2, half, LANES), BF),
        ah=((na, 2, half, LANES), BF), ay=((na, 2, half, LANES), BF),
        by=((nb, 4, 2, half, LANES), BF), bx=((nb, 4, half, LANES), BF), bzb=((nb, 3, half, LANES), BF),
        bzm=((nb, half, LANES), BF), bh=((nb, half, LANES), BF), bg=((nb, half, LANES), BF),
        czb=((nc, 3, 2, 2, half, LANES), BF), czm=((nc, 2, 2, half, LANES), BF), ch=((nc, 2, 2, half, LANES), BF),
        cx=((nc, 2, half, LANES), BF), cy=((nc, 2, half, LANES), BF), ds_in=((7, own, D), BF),
        vsh=((8, 24, 128), F32), vin=((7, 24, 128), F32), vrep=((4, 24, 128), F32),
    )
    sems = dict(
        w_sem=(8,), ss=(4,), sr=(4,), os=(10,), orr=(10,), ps=(n,), pr=(n, 3), zs=(n,), zr=(n, 2), cs=(1,), cr=(1,), fs=(3,)
    )
    vmem, hbm, smem = (pl.BlockSpec(memory_space=s) for s in (pltpu.VMEM, pl.ANY, pltpu.SMEM))
    shape = jax.ShapeDtypeStruct
    return pl.pallas_call(
        functools.partial(sum_kernel, INPUTS + SUM_OUT + list(table) + list(sems)),
        out_shape=(
            shape((rows, D), BF), shape((rows, D), F32), shape((UNITS * 16, 2, 2, half, LANES), BF), shape((own, D), F32), shape((24, 128), F32),
        ),
        in_specs=[vmem] * 4 + [smem] + [vmem] * 11 + [hbm] * 8,
        out_specs=(hbm, hbm, hbm, vmem, vmem),
        scratch_shapes=buffers(table) + [pltpu.SemaphoreType.DMA(dims) for dims in sems.values()],
        compiler_params=pltpu.CompilerParams(collective_id=0, has_side_effects=True, vmem_limit_bytes=VMEM_LIMIT),
        cost_estimate=pl.CostEstimate(flops=15 * 10**9, bytes_accessed=5 * 10**7, transcendentals=10**6),
    )(*small_inputs(args), *weight_inputs(args))


def place_kernel(result, d_hidden, fin, dstore, vec, *outs):
    (o_result, o_hidden, o_dstore, o_qkv, o_sbias, o_so, o_sob, o_n1, o_cq, o_cqb, o_ckv, o_cvb, o_co, o_cob, o_n2, o_fi, o_fib, o_fo, o_fob, o_n3) = outs
    o_result[...] = result[...]
    o_hidden[...] = d_hidden[...]
    o_dstore[...] = dstore[...]
    wide = {"qkv": o_qkv, "so": o_so, "cq": o_cq, "ckv": o_ckv, "co": o_co, "fi": o_fi}
    for i, (kind, part) in enumerate(PRODUCTS):
        for c in range(2):
            values = jnp.concatenate([fin[UNITS * i + unit, c] for unit in range(UNITS)], axis=1).astype(F32)
            if kind == "fo":
                begin = c * 2 * SHARD + (part // 2) * SHARD
                o_fo[begin : begin + SHARD, (part % 2) * PART : (part % 2 + 1) * PART] = values
            else:
                ref = wide[kind]
                begin = part * D + c * PART
                ref[:, begin : begin + PART] = values
    for ref, row in ((o_sbias, 0), (o_n1, 3), (o_n2, 8), (o_n3, 11)):
        ref[...] = vec[row : row + 2, 0:SHARD]
    for ref, row in ((o_sob, 2), (o_cqb, 5), (o_cvb, 6), (o_cob, 7), (o_fob, 10)):
        ref[...] = vec[row, 0:SHARD]
    for part in range(4):
        o_fib[pl.ds(part * SHARD, SHARD)] = vec[13 + part, 0:SHARD]


def place(result, d_hidden, fin, dstore, vec):
    shape = lambda *dims: jax.ShapeDtypeStruct(dims, F32)
    return pl.pallas_call(
        place_kernel,
        out_shape=(
            jax.ShapeDtypeStruct(result.shape, BF), shape(*d_hidden.shape), shape(*dstore.shape), shape(SHARD, 3 * D), shape(2, SHARD), shape(SHARD, D), shape(SHARD), shape(2, SHARD),
            shape(SHARD, D), shape(SHARD), shape(SHARD, 2 * D), shape(SHARD), shape(SHARD, D), shape(SHARD), shape(2, SHARD),
            shape(SHARD, FF), shape(FF // 8), shape(FF // 8, D), shape(SHARD), shape(2, SHARD),
        ),
        compiler_params=pltpu.CompilerParams(vmem_limit_bytes=VMEM_LIMIT),
    )(result, d_hidden, fin.reshape(UNITS * len(PRODUCTS), 2, SHARD, LANES), dstore, vec)


def sum_plainly(states, xt, act_t, dmat, dkv, dstore, vec):
    def total(value, dim):
        part = lax.psum_scatter(value, "blk", scatter_dimension=dim, tiled=True)
        return lax.psum(part.astype(BF), "rep").astype(F32)

    at_col = columns(False)

    def rows_of(start):
        return lax.slice_in_dim(xt, start, start + D, axis=0)

    def cols_of(start, width):
        return lax.slice_in_dim(dmat, start, start + width, axis=1)

    g_qkv = total(dot(rows_of(R_TOK), cols_of(at_col.proj, 3 * D)), 0)
    g_so = total(dot(rows_of(R_SMIX), cols_of(at_col.sb, D)), 0)
    g_cq = total(dot(rows_of(R_FIRST), cols_of(at_col.cq, D)), 0)
    g_co = total(dot(rows_of(R_CMIX), cols_of(at_col.cb, D)), 0)
    g_fi = total(dot(rows_of(R_SECOND), cols_of(at_col.inner, FF)), 0)
    g_fo = total(dot(act_t.reshape(FF, -1), cols_of(at_col.fb, D)), 0)
    g_ckv = total(dot_tn(states, dkv), 0)
    g_store = lax.psum_scatter(dstore.astype(F32), "blk", scatter_dimension=0, tiled=True)
    g_fib = total(vec[13:N_VEC].reshape(FF), 0)
    v = total(vec[:13].T, 0)
    two = lambda row: v[:, row : row + 2].T
    return (
        g_store, g_qkv, two(0), g_so, v[:, 2], two(3), g_cq, v[:, 5], g_ckv, v[:, 6], g_co, v[:, 7], two(8),
        g_fi, g_fib, g_fo, v[:, 10], two(11),
    )


def on_device(fast, *args):
    if fast:
        result, d_hidden, *grads = place(*run_sum(args))
    else:
        states_all = lax.all_gather(args[1][0], "blk", axis=0, tiled=True)
        result, d_hidden, *operands = run_plain(args, states_all)
        grads = sum_plainly(states_all, *operands)
    return (result[None, None], d_hidden[None, None], grads[0][None], *grads[1:])


def solution(mesh):
    fast = mesh.shape["blk"] == 8 and mesh.shape["rep"] == 4
    deep, flat = P("rep", "blk", None, None), P("rep", "blk", None)
    in_specs = (deep, flat, deep, deep, P("rep", "blk")) + (P(),) * 17 + (deep,)
    w, vec, two = P("blk", None), P("blk"), P(None, "blk")
    out_specs = (deep, deep, flat, w, two, w, vec, two, w, vec, w, vec, w, vec, two, w, vec, w, vec, two)
    return jax.shard_map(
        functools.partial(on_device, fast), mesh=mesh, in_specs=in_specs, out_specs=out_specs, check_vma=False
    )
```

```python
import functools
import typing

import jax
import jax.numpy as jnp
from jax import lax
from jax.experimental import pallas as pl
from jax.experimental.pallas import tpu as pltpu
from jax.sharding import PartitionSpec as P

D = 768
HEADS = 12
HD = 64
FF = 3072
EPS = 1e-05
NEG = -1e30
BF = jnp.bfloat16
F32 = jnp.float32
MESH = pl.DeviceIdType.MESH
VMEM_LIMIT = 63 * 2**20

N_VEC = 17
R_SECOND, R_TOK, R_SMIX, R_FIRST, R_CMIX, R_ALL = 0, 768, 1536, 2304, 3072, 3840
PART = 384
SHARD = D // 8
PRODUCTS = [("fo", i) for i in range(4)] + [("fi", i) for i in range(4)]
PRODUCTS += [("co", 0), ("cq", 0), ("ckv", 0), ("ckv", 1), ("so", 0), ("qkv", 0), ("qkv", 1), ("qkv", 2)]
LANES = 128
UNITS = PART // LANES
PIECES = [(i, 0, UNITS) for i in range(12)] + [(i, unit, 1) for i in range(12, 16) for unit in range(UNITS)]
WAYS = "BCAACABBBBABABBBCBAAABBB"
ORDER = (
    101, 102, 0, 1, 100, 103, 2, 3, 4, 5, 6, 7, 107, 106, 104, 8, 9, 10, 11, 105, 12, 13, 14, 15,
    16, 17, 18, 108, 19, 20, 21, 22, 110, 202, 200, 201, 122, 116, 203, 207, 111, 204, 205, 301, 23, 206, 109, 302,
    210, 120, 208, 113, 216, 304, 222, 123, 300, 402, 24, 303, 307, 114, 316, 401, 119, 211, 121, 305, 306, 403, 220, 115,
    112, 209, 310, 405, 308, 213, 400, 117, 404, 322, 223, 416, 407, 410, 502, 118, 219, 406, 500, 214, 320, 507, 501, 311,
    506, 408, 221, 212, 422, 420, 503, 319, 309, 215, 508, 313, 411, 522, 505, 419, 323, 312, 217, 218, 409, 511, 314, 504,
    413, 412, 516, 321, 423, 315, 510, 318, 317, 600, 509, 414, 607, 513, 421, 523, 606, 415, 520, 417, 418, 608, 622, 514,
    519, 521, 611, 515, 512, 517, 609, 613, 623, 518, 614, 621, 615, 617,
)
O_INNER, O_PROJ, O_SB, O_CQ, O_CB, O_FB, O_ALL = 0, 1536, 2688, 3072, 3456, 3840, 4608


class Columns(typing.NamedTuple):
    inner: int
    proj: int
    sb: int
    cq: int
    cb: int
    fb: int
    end: int


def columns(fast):
    return Columns(0, 0, 2304, 3072, 3840, 4608, 5376) if fast else Columns(0, 3072, 5376, 6144, 6912, 7680, 8448)


def dot(a, b):
    return lax.dot_general(a, b, (((1,), (0,)), ((), ())), preferred_element_type=F32)


def dot_nt(a, b):
    return lax.dot_general(a, b, (((1,), (1,)), ((), ())), preferred_element_type=F32)


def dot_tn(a, b):
    return lax.dot_general(a, b, (((0,), (0,)), ((), ())), preferred_element_type=F32)


def at(index, size):
    return pl.ds(pl.multiple_of(index * size, size), size)


def half_mask(half):
    lane = lax.broadcasted_iota(jnp.int32, (1, 2 * HD), 1)
    return ((lane >= HD) if half else (lane < HD)).astype(F32).astype(BF)


def total_row(values):
    return jnp.sum(values, axis=0, keepdims=True)


def gelu_and_slope(v):
    cdf = 0.5 * (1.0 + lax.erf(v * 0.7071067811865476))
    return v * cdf, cdf + v * (jnp.exp(-0.5 * v * v) * 0.3989422804014327)


def norm_rows(r):
    centered = r - jnp.mean(r, axis=-1, keepdims=True)
    rstd = lax.rsqrt(jnp.mean(centered * centered, axis=-1, keepdims=True) + EPS)
    return centered * rstd, rstd


def norm_rows_back(grad, xhat, rstd, gain):
    e = grad * gain
    mean_e = jnp.mean(e, axis=-1, keepdims=True)
    mean_x = jnp.mean(e * xhat, axis=-1, keepdims=True)
    return (e - mean_e - xhat * mean_x) * rstd


def attend(q_ref, k_ref, vt_ref, bias_ref, p_ref, mix_t_ref):
    scores = []
    for j in range(HEADS // 2):
        cols = slice(2 * HD * j, 2 * HD * (j + 1))
        q2, k2 = q_ref[:, cols], k_ref[:, cols]
        scores += [dot_nt(k2 * half_mask(half), q2) for half in range(2)]
    for h, st in enumerate(scores):
        st = st + bias_ref[...]
        e = jnp.exp(st - jnp.max(st, axis=0, keepdims=True))
        p_ref[h] = (e * (1.0 / jnp.sum(e, axis=0, keepdims=True))).astype(BF)
    for h in range(HEADS):
        rows = slice(HD * h, HD * (h + 1))
        mix_t_ref[rows, :] = dot(vt_ref[rows, :], p_ref[h]).astype(BF)


def attend_back(p_ref, dmix_ref, q_ref, v_ref, kt_ref, dq_t_ref, put, begin, end):
    parts = []
    for j in range(begin, end):
        cols = slice(2 * HD * j, 2 * HD * (j + 1))
        dm2, q2, v2 = dmix_ref[:, cols], q_ref[:, cols], v_ref[:, cols]
        parts += [(2 * j + half, dm2 * half_mask(half), q2 * half_mask(half), dot_nt(v2 * half_mask(half), dm2)) for half in range(2)]
    grads = []
    for h, dm, q, dp in parts:
        p = p_ref[h].astype(F32)
        t = p * dp
        grads.append((t - p * jnp.sum(t, axis=0, keepdims=True)).astype(BF))
    for n, (h, dm, q, dp) in enumerate(parts):
        dq_t_ref[HD * h : HD * (h + 1), :] = dot(kt_ref[HD * h : HD * (h + 1), :], grads[n]).astype(BF)
    for n in range(0, len(parts), 2):
        (h, dm0, q0, _), (_, dm1, q1, _) = parts[n : n + 2]
        put(h // 2, dot(grads[n], q0) + dot(grads[n + 1], q1), dot(p_ref[h], dm0) + dot(p_ref[h + 1], dm1))


class Refs:
    def __init__(self, names, refs):
        for name, ref in zip(names, refs, strict=True):
            setattr(self, name, ref)


class Inputs(typing.NamedTuple):
    tokens: typing.Any
    states: typing.Any
    retrieved: typing.Any
    live: typing.Any
    lengths: typing.Any
    self_bias: typing.Any
    self_out_bias: typing.Any
    norm1: typing.Any
    cq_bias: typing.Any
    cv_bias: typing.Any
    co_bias: typing.Any
    norm2: typing.Any
    fi_bias: typing.Any
    fo_bias: typing.Any
    norm3: typing.Any
    cotangent: typing.Any
    h_qkv: typing.Any
    h_qkv6: typing.Any
    h_so: typing.Any
    h_cq: typing.Any
    h_ckv: typing.Any
    h_co: typing.Any
    h_fi: typing.Any
    h_fo: typing.Any


INPUTS = list(Inputs._fields)


def layer(m, net, at_col):
    rows = m.tokens.shape[0]
    length = m.lengths[0, 0]
    scale = HD**-0.5
    xt, dmat, vec = m.xt, m.dmat, m.vec
    copies = {}
    order = [("so", m.h_so, m.w_so), ("cq", m.h_cq, m.w_cq), ("ckv", m.h_ckv, m.w_ckv), ("co", m.h_co, m.w_co), ("fi", m.h_fi, m.w_fi)]

    def fetch_units(src, first, count, sem):
        for i in range(count):
            pltpu.make_async_copy(src(i), m.ring.at[first + i], sem).start()

    def have_units(first, count, sem):
        here = m.ring.at[first : first + count]
        pltpu.make_async_copy(here, here, sem).wait()

    def weight(slot):
        return jnp.concatenate([m.ring[UNITS * slot + unit].reshape(D, LANES) for unit in range(UNITS)], axis=1)

    fetch_units(lambda i: m.h_qkv6.at[:, :, :, :, i * LANES : (i + 1) * LANES], 0, 18, m.w_sem.at[6])
    if net:
        net.greet()

    def piece(name):
        return slice(getattr(at_col, name), getattr(at_col, name) + D)

    xt[R_TOK : R_TOK + D, :] = m.tokens[...].T
    key_at = lax.broadcasted_iota(jnp.int32, (rows, rows), 0)
    query_at = lax.broadcasted_iota(jnp.int32, (rows, rows), 1)
    m.bias_s[...] = jnp.where((key_at <= query_at) & (key_at < length), 0.0, NEG)
    if net:
        net.begin()
    topk = m.retrieved.shape[0]
    slots = m.bias_c.shape[0]
    slot_rank = lax.broadcasted_iota(jnp.int32, (topk, rows), 0)
    chosen = jnp.where((m.live[...] > 0) | (slot_rank == 0), m.retrieved[...], -1)

    def mask_rows(i, _):
        ids = lax.broadcasted_iota(jnp.int32, (32, rows), 0) + i * 32
        hit = jnp.zeros((32, rows), jnp.bool_)
        for j in range(topk):
            hit = hit | (ids == chosen[j : j + 1, :])
        m.bias_c[at(i, 32), :] = jnp.where(hit, 0.0, NEG)
        return 0

    lax.fori_loop(0, slots // 32, mask_rows, 0)

    for i, (ref, bias) in enumerate(((m.q, 0), (m.q, 0), (m.k, None), (m.k, None), (m.v, 1), (m.v, 1))):
        if i == 0:
            have_units(0, 18, m.w_sem.at[6])
        cols = slice((i % 2) * PART, (i % 2 + 1) * PART)
        got = dot(m.tokens[...], weight(i))
        if bias is not None:
            got = got + m.self_bias[bias : bias + 1, cols]
        got = got.astype(BF)
        ref[:, cols] = got * scale if bias == 0 else got
    for i, (name, src, dst) in enumerate(order):
        copies[name] = pltpu.make_async_copy(src, dst, m.w_sem.at[i])
        copies[name].start()
    fetch_units(lambda i: m.h_fo.at[i // 6, :, :, :, :, i % 6 * LANES : (i % 6 + 1) * LANES], 24, 24, m.w_sem.at[7])
    m.vt[...] = m.v[...].T
    attend(m.q, m.k, m.vt, m.bias_s, m.p_s, xt.at[R_SMIX : R_SMIX + D])
    m.vt[...] = m.k[...].T * scale
    copies["so"].wait()
    if net:
        net.swap_rows("smix")
    m.mix_b[...] = xt[R_SMIX : R_SMIX + D, :].T
    m.acc[...] = dot(m.mix_b[...], m.w_so[...])

    def ln1(rs):
        xhat, rstd = norm_rows(m.tokens[rs, :].astype(F32) + m.acc[rs, :] + m.self_out_bias[...][None, :])
        m.xhat1[rs, :] = xhat
        m.rstd1[rs, :] = rstd
        m.sec_b[rs, :] = (xhat * m.norm1[0:1, :] + m.norm1[1:2, :]).astype(BF)

    ln1(slice(0, rows))
    xt[R_FIRST : R_FIRST + D, :] = m.sec_b[...].T
    if net:
        net.swap_rows("first")

    copies["cq"].wait()
    m.k[...] = (dot(m.sec_b[...], m.w_cq[...]) + m.cq_bias[...][None, :]).astype(BF) * scale
    copies["ckv"].wait()
    if net:
        net.have_states()
    states = m.all_states[...].reshape(slots, D)
    m.sk[...] = dot(states, m.w_ckv[:, :D]).astype(BF)
    m.sv[...] = (dot(states, m.w_ckv[:, D:]) + m.cv_bias[...][None, :]).astype(BF)
    m.svt[...] = m.sv[...].T
    attend(m.k, m.sk, m.svt, m.bias_c, m.p_c, xt.at[R_CMIX : R_CMIX + D])
    m.svt[...] = m.sk[...].T * scale
    copies["co"].wait()
    if net:
        net.swap_rows("cmix")
    m.mix_b[...] = xt[R_CMIX : R_CMIX + D, :].T
    m.acc[...] = dot(m.mix_b[...], m.w_co[...])

    def ln2(rs):
        first = m.xhat1[rs, :] * m.norm1[0:1, :] + m.norm1[1:2, :]
        xhat, rstd = norm_rows(first + m.acc[rs, :] + m.co_bias[...][None, :])
        m.xhat2[rs, :] = xhat
        m.rstd2[rs, :] = rstd
        m.sec_b[rs, :] = (xhat * m.norm2[0:1, :] + m.norm2[1:2, :]).astype(BF)

    ln2(slice(0, rows))
    xt[R_SECOND : R_SECOND + D, :] = m.sec_b[...].T
    if net:
        net.swap_rows("second")

    copies["fi"].wait()
    have_units(24, 24, m.w_sem.at[7])
    for j in range(FF // D):
        cols = slice(j * D, (j + 1) * D)
        m.acc2[...] = dot(m.sec_b[...], m.w_fi[:, cols])
        bias = m.fi_bias[cols][None, :]

        def gelu(rs):
            a, s = gelu_and_slope(m.acc2[rs, :] + bias)
            m.mix_b[rs, :] = a.astype(BF)
            m.slope[rs, cols] = s.astype(BF)

        gelu(slice(0, rows))
        m.act_t[2 * j : 2 * j + 2] = m.mix_b[...].T.reshape(2, 2, 2 * SHARD, rows)
        if net:
            net.swap_act(j)
        for part in range(2):
            got = dot(m.mix_b[...], weight(8 + 2 * j + part))
            here = slice(part * PART, (part + 1) * PART)
            m.acc[:, here] = got if j == 0 else m.acc[:, here] + got

    def ln3(rs):
        second = m.xhat2[rs, :] * m.norm2[0:1, :] + m.norm2[1:2, :]
        xhat, rstd = norm_rows(second + m.acc[rs, :] + m.fo_bias[...][None, :])
        m.result[rs, :] = (xhat * m.norm3[0:1, :] + m.norm3[1:2, :]).astype(BF)
        place = lax.broadcasted_iota(jnp.int32, (rows, 1), 0)
        g = m.cotangent[rs, :].astype(F32) * jnp.where(place < length, 1.0, 0.0)
        d = norm_rows_back(g, xhat, rstd, m.norm3[0:1, :])
        m.d_res[rs, :] = d
        db = d.astype(BF)
        dmat[rs, piece("fb")] = db
        return total_row(g * xhat), total_row(g), total_row(db.astype(F32))

    vec[N_VEC:, :] = jnp.zeros((vec.shape[0] - N_VEC, D), F32)
    vec[11:12, :], vec[12:13, :], vec[10:11, :] = ln3(slice(0, rows))
    if net:
        net.swap("fb")

    steps = []

    def feed_back(j):
        cols = slice(j * D, (j + 1) * D)
        inner = slice(at_col.inner + j * D, at_col.inner + (j + 1) * D)
        left, right = (dmat[:, at_col.fb + part * PART : at_col.fb + (part + 1) * PART] for part in range(2))
        m.acc2[...] = dot_nt(left, weight(8 + 2 * j)) + dot_nt(right, weight(9 + 2 * j))

        def inner_rows(rs):
            d = (m.slope[rs, cols].astype(F32) * m.acc2[rs, :]).astype(BF)
            dmat[rs, inner] = d
            return total_row(d.astype(F32))

        vec[13 + j : 14 + j, :] = inner_rows(slice(0, rows))
        if net:
            net.swap("inner", j)

    def feed_back_x(j):
        inner = slice(at_col.inner + j * D, at_col.inner + (j + 1) * D)
        got = dot_nt(dmat[:, inner], m.w_fi[:, j * D : (j + 1) * D])
        m.acc[...] = (m.d_res[...] if j == 0 else m.acc[...]) + got

    for j in range(FF // D):
        steps += [functools.partial(feed_back, j), functools.partial(feed_back_x, j)]

    def norm_back(xhat_ref, rstd_ref, norm, name):
        def block(rs):
            g, xhat = m.acc[rs, :], xhat_ref[rs, :]
            d = norm_rows_back(g, xhat, rstd_ref[rs, :], norm[0:1, :])
            m.d_res[rs, :] = d
            db = d.astype(BF)
            dmat[rs, piece(name)] = db
            return total_row(g * xhat), total_row(g), total_row(db.astype(F32))

        sums = block(slice(0, rows))
        if net:
            net.swap(name)
        return sums

    def back_norm2():
        copies["qkv"] = pltpu.make_async_copy(m.h_qkv, m.w_fi.at[:, 0 : 3 * D], m.w_sem.at[5])
        copies["qkv"].start()
        vec[8:9, :], vec[9:10, :], vec[7:8, :] = norm_back(m.xhat2, m.rstd2, m.norm2, "cb")

    def back_cross_out():
        m.mix_b[...] = dot_nt(dmat[:, piece("cb")], m.w_co[...]).astype(BF)

    def put_store(j, dk, dv):
        cols = slice(2 * HD * j, 2 * HD * (j + 1))
        m.dkv[:, cols] = dk.astype(BF)
        m.dkv[:, D + 2 * HD * j : D + 2 * HD * (j + 1)] = dv.astype(BF)
        vec[6:7, cols] = total_row(dv)

    def back_cross(part):
        attend_back(m.p_c, m.mix_b, m.k, m.sv, m.svt, m.dqt, put_store, 2 * part, 2 * part + 2)
        if net and part == 2:
            net.swap("dkv", 0)
            net.swap("dkv", 1)

    def back_query():
        dq = m.dqt[...].T
        dmat[:, piece("cq")] = dq
        if net:
            net.swap("cq")
        vec[5:6, :] = total_row(dq.astype(F32))

    def back_store():
        m.dstore[...] = dot_nt(m.dkv[...], m.w_ckv[...]).astype(BF).reshape(m.dstore.shape)
        if net:
            net.send_dstore()

    def back_first():
        m.acc[...] = m.d_res[...] + dot_nt(dmat[:, piece("cq")], m.w_cq[...])

    def back_norm1():
        if net:
            net.inner_gone()
        vec[3:4, :], vec[4:5, :], vec[2:3, :] = norm_back(m.xhat1, m.rstd1, m.norm1, "sb")

    def back_self_out():
        m.mix_b[...] = dot_nt(dmat[:, piece("sb")], m.w_so[...]).astype(BF)

    def put_self(j, dk, dv):
        dvb = dv.astype(BF)
        begin = at_col.proj + D + 2 * HD * j
        dmat[:, begin : begin + 2 * HD] = dk.astype(BF)
        dmat[:, begin + D : begin + D + 2 * HD] = dvb
        vec[1:2, 2 * HD * j : 2 * HD * (j + 1)] = total_row(dvb.astype(F32))

    def back_self(part):
        attend_back(m.p_s, m.mix_b, m.q, m.v, m.vt, m.dqt, put_self, 2 * part, 2 * part + 2)
        if net and part == 2:
            net.swap("proj", 1)
            net.swap("proj", 2)

    def back_proj():
        dq = m.dqt[...].T
        dmat[:, at_col.proj : at_col.proj + D] = dq
        if net:
            net.swap("proj", 0)
        vec[0:1, :] = total_row(dq.astype(F32))
        if net:
            net.send_vec()

    def back_hidden():
        copies["qkv"].wait()
        m.acc[...] = m.d_res[...] + dot_nt(dmat[:, at_col.proj : at_col.proj + 3 * D], m.w_fi[:, 0 : 3 * D])
        if net:
            net.keep(m.acc, m.d_hidden, m.fs.at[1])
            net.keep(m.result, m.result_out, m.fs.at[2])

    steps += [back_norm2, back_cross_out] + [functools.partial(back_cross, part) for part in range(3)]
    steps += [back_query, back_store, back_first, back_norm1, back_self_out] + [functools.partial(back_self, part) for part in range(3)]
    steps += [back_proj, back_hidden]
    if net:
        steps += [net.small_sums, net.small_total]
        steps += [functools.partial(net.make, i) for i in range(len(PRODUCTS))]
        for number in ORDER:
            if number < 100:
                steps[number]()
            else:
                net.step(number // 100 - 1, number % 100)
        net.finish()
    else:
        for step in steps:
            step()


def weight_inputs(args):
    self_qkv, self_out, cross_q, cross_kv, cross_out, ffn_in, ffn_out = (args[i] for i in (5, 7, 10, 12, 14, 17, 19))
    return (self_qkv, self_qkv.reshape(4, 2, 2, D // 16, 3 * D), self_out, cross_q, cross_kv, cross_out, ffn_in,
            ffn_out.reshape(FF // D, 4, 2, 2, D // 16, D))


def small_inputs(args):
    (hidden, store, retrieved, live, lengths, _, self_bias, _, self_out_bias, norm1, _, cross_q_bias,
     _, cross_v_bias, _, cross_out_bias, norm2, _, ffn_in_bias, _, ffn_out_bias, norm3, cotangent) = args
    return (
        hidden[0, 0], store[0], jnp.swapaxes(retrieved[0, 0], 0, 1), jnp.swapaxes(live[0, 0], 0, 1), lengths, self_bias,
        self_out_bias, norm1, cross_q_bias, cross_v_bias, cross_out_bias, norm2, ffn_in_bias, ffn_out_bias, norm3, cotangent[0, 0],
    )


def layer_scratch(rows, slots):
    wide = (rows, D)
    return dict(
        ring=((UNITS * 16, 4, 2, 2, D // 16, LANES), BF), w_so=((D, D), BF), w_cq=((D, D), BF), w_ckv=((D, 2 * D), BF),
        w_co=((D, D), BF), w_fi=((D, FF), BF),
        q=(wide, BF), k=(wide, BF), v=(wide, BF), vt=((D, rows), BF), bias_s=((rows, rows), F32),
        p_s=((HEADS, rows, rows), BF), sk=((slots, D), BF), sv=((slots, D), BF), svt=((D, slots), BF),
        bias_c=((slots, rows), F32), p_c=((HEADS, slots, rows), BF), mix_b=(wide, BF),
        acc=(wide, F32), acc2=(wide, F32), xhat1=(wide, F32), xhat2=(wide, F32),
        sec_b=(wide, BF), slope=((rows, FF), BF), d_res=(wide, F32), dqt=((D, rows), BF),
        rstd1=((rows, 1), F32), rstd2=((rows, 1), F32),
    )


def buffers(table):
    return [pltpu.VMEM(dims, kind) for dims, kind in table.values()]


PLAIN_OUT = ["result", "acc", "xt", "act_t", "dmat", "dkv", "dstore", "vec"]


def plain_kernel(names, *refs):
    layer(Refs(names, refs), None, columns(False))


def run_plain(args, states_all):
    rows, slots = args[0].shape[2], states_all.shape[0]
    at_col = columns(False)
    table = layer_scratch(rows, slots)
    del table["acc"]
    vmem, hbm, smem = (pl.BlockSpec(memory_space=s) for s in (pltpu.VMEM, pl.ANY, pltpu.SMEM))
    shape = jax.ShapeDtypeStruct
    names = INPUTS + PLAIN_OUT + list(table) + ["w_sem"]
    names[names.index("states")] = "all_states"
    small = small_inputs(args)
    outs = pl.pallas_call(
        functools.partial(plain_kernel, names),
        out_shape=(
            shape((rows, D), BF), shape((rows, D), F32), shape((R_ALL, rows), BF), shape((8, 2, 2 * SHARD, rows), BF),
            shape((rows, at_col.end), BF), shape((slots, 2 * D), BF), shape((slots, D), BF), shape((24, D), F32),
        ),
        in_specs=[vmem] * 4 + [smem] + [vmem] * 11 + [hbm] * 8,
        out_specs=(vmem,) * 8,
        scratch_shapes=buffers(table) + [pltpu.SemaphoreType.DMA((8,))],
        compiler_params=pltpu.CompilerParams(vmem_limit_bytes=VMEM_LIMIT),
    )(small[0], states_all, *small[2:], *weight_inputs(args))
    return outs


class Net:
    def __init__(self, m, at_col):
        self.m, self.at_col = m, at_col
        b, r = lax.axis_index("blk"), lax.axis_index("rep")
        self.b, self.r = b, r
        self.z, self.x, self.y, self.c = b // 2, b % 2, r // 2, r % 2
        z, x, y, c = self.z, self.x, self.y, self.c
        self.at_x = (z * 2 + 1 - x, r)
        self.at_y = (b, (1 - y) * 2 + c)
        self.at_c = (b, y * 2 + 1 - c)
        side = z // 2
        self.side, self.is_end = side, jnp.logical_or(z == 0, z == 3)
        self.at_mid, self.at_end = ((1 + side) * 2 + x, r), (3 * side * 2 + x, r)
        self.at_near, self.at_far = ((2 - side) * 2 + x, r), (3 * (1 - side) * 2 + x, r)
        self.at_blk = [(lax.rem(b + step, 8), r) for step in range(1, 8)]
        self.at_rep = [(b, lax.rem(r + step, 4)) for step in range(1, 4)]
        self.here, self.swapped = [], []
        self.steps, self.chain = {}, []
        self.span, self.own, taken = [], [], dict.fromkeys(WAYS, 0)
        for way, (product, unit, units) in zip(WAYS, PIECES, strict=True):
            self.span.append(slice(taken[way], taken[way] + units))
            self.own.append(slice(UNITS * product + unit, UNITS * product + unit + units))
            taken[way] += units
        self.made = []

    def copy(self, src, dst, s_sem, r_sem, device):
        return pltpu.make_async_remote_copy(
            src_ref=src, dst_ref=dst, send_sem=s_sem, recv_sem=r_sem, device_id=device, device_id_type=MESH
        )

    def send(self, *args):
        copy = self.copy(*args)
        copy.start()
        return copy

    def sized(self, ref, s_sem, r_sem):
        return self.copy(ref, ref, s_sem, r_sem, self.at_c)

    def greet(self):
        barrier = pltpu.get_barrier_semaphore()
        for device in self.at_blk + self.at_rep:
            pl.semaphore_signal(barrier, inc=1, device_id=device, device_id_type=MESH)

    def begin(self):
        m = self.m
        m.all_states[self.b] = m.states[...]
        pl.semaphore_wait(pltpu.get_barrier_semaphore(), len(self.at_blk) + len(self.at_rep))
        for device in self.at_blk:
            self.send(m.states, m.all_states.at[self.b], m.ss.at[0], m.sr.at[0], device)
        self.swap_rows("tok")

    def have_states(self):
        m = self.m
        self.sized(m.all_states.at[0:7], m.ss.at[0], m.sr.at[0]).wait_recv()
        self.trade("states", m.all_states, m.states_p)

    def group(self, name):
        m = self.m
        part = lambda start, width: m.d_p.at[:, start : start + width]
        table = {
            "rows": m.xt_p, "act": m.act_p, "fb": part(O_FB, D), "inner": part(O_INNER, 4 * PART), "cb": part(O_CB, PART),
            "cq": part(O_CQ, PART), "dkv": m.dkv_p, "sb": part(O_SB, PART), "proj": part(O_PROJ, 3 * PART), "states": m.states_p,
        }
        i = list(table).index(name)
        return table[name], m.os.at[i], m.orr.at[i]

    def trade(self, name, src, dst):
        _, s_sem, r_sem = self.group(name)
        self.send(src, dst, s_sem, r_sem, self.at_c)
        if name not in self.swapped:
            self.swapped.append(name)

    def need(self, *names):
        for name in names:
            if name not in self.here:
                self.sized(*self.group(name)).wait_recv()
                self.here.append(name)

    def swap_rows(self, name):
        row = {"tok": R_TOK, "smix": R_SMIX, "first": R_FIRST, "cmix": R_CMIX, "second": R_SECOND}[name]
        self.trade("rows", self.m.xt.at[row : row + D], self.m.xt_p.at[row : row + D])

    def swap_act(self, j):
        here = slice(2 * j, 2 * j + 2)
        self.trade("act", self.m.act_t.at[here, 1 - self.c], self.m.act_p.at[here])

    def half(self, start, who):
        return pl.ds(pl.multiple_of(start + who * PART, 128), PART)

    def operand(self, name, part):
        m, at_col = self.m, self.at_col
        if name == "dkv":
            return m.dkv, part * D, m.dkv_p, part * PART
        place = {"inner": O_INNER, "proj": O_PROJ, "sb": O_SB, "cq": O_CQ, "cb": O_CB}[name]
        return m.dmat, getattr(at_col, name) + part * D, m.d_p, place + part * PART

    def swap(self, name, part=0):
        m = self.m
        if name == "fb":
            start = self.at_col.fb
            self.trade("fb", m.dmat.at[:, start : start + D], m.d_p.at[:, O_FB : O_FB + D])
            return
        ref, start, there, place = self.operand(name, part)
        self.trade(name, ref.at[:, self.half(start, 1 - self.c)], there.at[:, place : place + PART])

    def product(self, i):
        m = self.m
        kind, part = PRODUCTS[i]
        if kind == "fo":
            self.need("fb", "act")
            up = slice((part // 2) * SHARD, (part // 2 + 1) * SHARD)
            left = m.act_t[:, self.c, up, :].reshape(D, -1)
            left_p = m.act_p[:, up, :].reshape(D, -1)
            begin = (part % 2) * PART
            right = m.dmat[:, self.at_col.fb + begin : self.at_col.fb + begin + PART]
            right_p = m.d_p[:, O_FB + begin : O_FB + begin + PART]
        else:
            name, row = {"fi": ("inner", R_SECOND), "co": ("cb", R_CMIX), "cq": ("cq", R_FIRST), "ckv": ("dkv", 0),
                         "so": ("sb", R_SMIX), "qkv": ("proj", R_TOK)}[kind]
            self.need(name, "states" if kind == "ckv" else "rows")
            ref, start, there, place = self.operand(name, part)
            right = ref[:, self.half(start, self.c)]
            right_p = there[:, place : place + PART]
            if kind == "ckv":
                left = m.all_states[...].reshape(-1, D).T
                left_p = m.states_p[...].reshape(-1, D).T
            else:
                left, left_p = m.xt[row : row + D, :], m.xt_p[row : row + D, :]
        total = (dot(left, right) + dot(left_p, right_p)).astype(BF)
        for unit in range(UNITS):
            m.ring[UNITS * i + unit] = total[:, unit * LANES : (unit + 1) * LANES].reshape(4, 2, 2, SHARD // 2, LANES)

    def make(self, i):
        if i not in self.made:
            self.made.append(i)
            self.product(i)

    def step(self, stage, i):
        if stage == 0:
            self.make(PIECES[i][0])
        ways = {
            "A": (self.a0, self.a1, self.a2, self.a3, self.a4),
            "B": (self.b0, self.b1, self.b2, self.b3, self.b4, self.b5),
            "C": (self.c0, self.c1, self.c2, self.c3, self.c4),
        }
        ways[WAYS[i]][stage](i, self.span[i], self.own[i])

    def post(self, i, src, dst, device):
        sent = self.steps.setdefault(i, [])
        if sent:
            sent[-1].wait_send()
        sent.append(self.send(src, dst, self.m.ps.at[i], self.m.pr.at[i, len(sent)], device))

    def arrived(self, i):
        self.steps[i][-1].wait_recv()

    def z_send(self, i, part, zb):
        m, others, edge = self.m, pl.ds(1 - self.side, 3), 3 * self.side

        @pl.when(self.is_end)
        def _():
            self.send(part.at[:, others], zb, m.zs.at[i], m.zr.at[i, 0], self.at_mid)

        @pl.when(jnp.logical_not(self.is_end))
        def _():
            self.send(part.at[:, edge], zb.at[:, 0], m.zs.at[i], m.zr.at[i, 0], self.at_end)

    def z_pass(self, i, part, zb, zm):
        m, side = self.m, self.side
        far, near = 2 * (1 - side), 1

        @pl.when(jnp.logical_not(self.is_end))
        def _():
            self.sized(zb, m.zs.at[i], m.zr.at[i, 0]).wait_recv()
            zb[:, far] = zb[:, far] + part[:, 3 * (1 - side)]
            self.send(zb.at[:, far], zb.at[:, 1], m.zs.at[i], m.zr.at[i, 1], self.at_far)
            zb[:, near] = zb[:, near] + part[:, 2 - side]
            self.send(zb.at[:, near], zm, m.zs.at[i], m.zr.at[i, 1], self.at_near)

    def z_sum(self, i, part, zb, zm, out):
        m, side = self.m, self.side

        @pl.when(self.is_end)
        def _():
            self.sized(zm, m.zs.at[i], m.zr.at[i, 0]).wait_recv()
            self.sized(zm, m.zs.at[i], m.zr.at[i, 1]).wait_recv()
            out[...] = (part[:, self.z].astype(F32) + zb[:, 0].astype(F32) + zb[:, 1].astype(F32)).astype(BF)

        @pl.when(jnp.logical_not(self.is_end))
        def _():
            self.sized(zm, m.zs.at[i], m.zr.at[i, 1]).wait_recv()
            out[...] = (part[:, self.z].astype(F32) + zb[:, 2 * side].astype(F32) + zm[...].astype(F32)).astype(BF)

        self.chain.append((zb, i))

    def last(self, ref, there):
        m = self.m
        pltpu.make_async_copy(ref, there, m.fs.at[0]).start()
        self.send(ref, there, m.cs.at[0], m.cr.at[0], self.at_c)

    def a0(self, i, at, own):
        self.post(i, self.m.ring.at[own, :, 1 - self.x], self.m.ax.at[at], self.at_x)

    def a1(self, i, at, own):
        m = self.m
        self.arrived(i)
        m.ax[at] = m.ax[at] + m.ring[own, :, self.x]
        self.z_send(i, m.ax.at[at], m.azb.at[at])

    def a2(self, i, at, own):
        self.z_pass(i, self.m.ax.at[at], self.m.azb.at[at], self.m.azm.at[at])

    def a3(self, i, at, own):
        m = self.m
        self.z_sum(i, m.ax.at[at], m.azb.at[at], m.azm.at[at], m.ah.at[at])
        self.post(i, m.ah.at[at], m.ay.at[at], self.at_y)

    def a4(self, i, at, own):
        m = self.m
        self.arrived(i)
        m.ay[at] = m.ay[at] + m.ah[at]
        self.last(m.ay.at[at], m.fin.at[own, self.c])

    def b0(self, i, at, own):
        self.post(i, self.m.ring.at[own, :, :, 1 - self.y], self.m.by.at[at], self.at_y)

    def b1(self, i, at, own):
        m = self.m
        self.arrived(i)
        m.by[at] = m.by[at] + m.ring[own, :, :, self.y]
        self.post(i, m.by.at[at, :, 1 - self.x], m.bx.at[at], self.at_x)

    def b2(self, i, at, own):
        m = self.m
        self.arrived(i)
        m.bx[at] = m.bx[at] + m.by[at, :, self.x]
        self.z_send(i, m.bx.at[at], m.bzb.at[at])

    def b3(self, i, at, own):
        self.z_pass(i, self.m.bx.at[at], self.m.bzb.at[at], self.m.bzm.at[at])

    def b4(self, i, at, own):
        m = self.m
        self.z_sum(i, m.bx.at[at], m.bzb.at[at], m.bzm.at[at], m.bh.at[at])
        self.post(i, m.bh.at[at], m.bg.at[at], self.at_y)
        self.last(m.bh.at[at], m.fin.at[own, self.c, self.y])

    def b5(self, i, at, own):
        self.arrived(i)
        self.last(self.m.bg.at[at], self.m.fin.at[own, self.c, 1 - self.y])

    def c0(self, i, at, own):
        self.z_send(i, self.m.ring.at[own], self.m.czb.at[at])

    def c1(self, i, at, own):
        self.z_pass(i, self.m.ring.at[own], self.m.czb.at[at], self.m.czm.at[at])

    def c2(self, i, at, own):
        m = self.m
        self.z_sum(i, m.ring.at[own], m.czb.at[at], m.czm.at[at], m.ch.at[at])
        self.post(i, m.ch.at[at, 1 - self.x], m.cx.at[at], self.at_x)

    def c3(self, i, at, own):
        m = self.m
        self.arrived(i)
        m.cx[at] = m.cx[at] + m.ch[at, self.x]
        self.post(i, m.cx.at[at], m.cy.at[at], self.at_y)

    def c4(self, i, at, own):
        m = self.m
        self.arrived(i)
        m.cy[at] = m.cy[at] + m.cx[at]
        self.last(m.cy.at[at], m.fin.at[own, self.c])

    def keep(self, src, dst, sem):
        pltpu.make_async_copy(src, dst, sem).start()

    def inner_gone(self):
        self.sized(*self.group("inner")).wait_send()

    def send_dstore(self):
        m = self.m
        for i, device in enumerate(self.at_blk):
            self.send(m.dstore.at[device[0]], m.ds_in.at[i], m.ss.at[1], m.sr.at[1], device)

    def send_vec(self):
        m, vec = self.m, self.m.vec
        m.vsh[...] = jnp.zeros(m.vsh.shape, F32)
        for s in range(8):
            m.vsh[s, 0:13, 0:SHARD] = vec[0:13, s * SHARD : (s + 1) * SHARD]
            for part in range(4):
                begin = 4 * SHARD * s + SHARD * part
                row, col = 13 + begin // D, begin % D
                m.vsh[s, 13 + part : 14 + part, 0:SHARD] = vec[row : row + 1, col : col + SHARD]
        for i, device in enumerate(self.at_blk):
            self.send(m.vsh.at[device[0]], m.vin.at[i], m.ss.at[2], m.sr.at[2], device)

    def finish(self):
        m = self.m
        for name in self.swapped:
            self.need(name)
            if name != "inner":
                self.sized(*self.group(name)).wait_send()
        for sent in self.steps.values():
            sent[-1].wait_send()
        for zb, i in self.chain:
            self.sized(zb, m.zs.at[i], m.zr.at[i, 0]).wait_send()
        for k, ref in enumerate((m.all_states.at[0:7], m.ds_in, m.vin, m.vrep.at[0:3])):
            self.sized(ref, m.ss.at[k], m.sr.at[k]).wait_send()
        half = m.fin.at[:, self.c]
        self.sized(half, m.cs.at[0], m.cr.at[0]).wait()
        pltpu.make_async_copy(half, half, m.fs.at[0]).wait()
        pltpu.make_async_copy(m.acc, m.d_hidden, m.fs.at[1]).wait()
        pltpu.make_async_copy(m.result, m.result_out, m.fs.at[2]).wait()

    def small_total(self):
        m = self.m
        self.sized(m.vrep.at[0:3], m.ss.at[3], m.sr.at[3]).wait_recv()
        m.vec_out[...] = (m.vrep[0] + m.vrep[1]) + (m.vrep[2] + m.vrep[3])

    def small_sums(self):
        m = self.m
        self.sized(m.ds_in, m.ss.at[1], m.sr.at[1]).wait_recv()
        total = m.dstore[self.b].astype(F32)
        for i in range(7):
            total = total + m.ds_in[i].astype(F32)
        m.dstore_out[...] = total
        self.sized(m.vin, m.ss.at[2], m.sr.at[2]).wait_recv()
        total = m.vsh[self.b]
        for i in range(7):
            total = total + m.vin[i]
        m.vrep[self.r] = total
        for device in self.at_rep:
            self.send(m.vrep.at[self.r], m.vrep.at[self.r], m.ss.at[3], m.sr.at[3], device)


SUM_OUT = ["result_out", "d_hidden", "fin", "dstore_out", "vec_out"]


def sum_kernel(names, *refs):
    m, at_col = Refs(names, refs), columns(True)
    layer(m, Net(m, at_col), at_col)


def run_sum(args):
    rows, own = args[0].shape[2], args[1].shape[1]
    slots = 8 * own
    n, half = len(PIECES), SHARD // 2
    na, nb, nc = (sum(piece[2] for piece, its in zip(PIECES, WAYS, strict=True) if its == way) for way in "ABC")
    table = layer_scratch(rows, slots)
    table.update(
        result=((rows, D), BF), xt=((R_ALL, rows), BF), xt_p=((R_ALL, rows), BF), act_t=((8, 2, 2 * SHARD, rows), BF),
        act_p=((8, 2 * SHARD, rows), BF), dmat=((rows, columns(True).end), BF), d_p=((rows, O_ALL), BF),
        dkv=((slots, 2 * D), BF), dkv_p=((slots, D), BF), dstore=((8, own, D), BF), vec=((24, D), F32),
        all_states=((8, own, D), BF), states_p=((8, own, D), BF),
        ax=((na, 4, 2, half, LANES), BF), azb=((na, 3, 2, half, LANES), BF), azm=((na, 2, half, LANES), BF),
        ah=((na, 2, half, LANES), BF), ay=((na, 2, half, LANES), BF),
        by=((nb, 4, 2, half, LANES), BF), bx=((nb, 4, half, LANES), BF), bzb=((nb, 3, half, LANES), BF),
        bzm=((nb, half, LANES), BF), bh=((nb, half, LANES), BF), bg=((nb, half, LANES), BF),
        czb=((nc, 3, 2, 2, half, LANES), BF), czm=((nc, 2, 2, half, LANES), BF), ch=((nc, 2, 2, half, LANES), BF),
        cx=((nc, 2, half, LANES), BF), cy=((nc, 2, half, LANES), BF), ds_in=((7, own, D), BF),
        vsh=((8, 24, 128), F32), vin=((7, 24, 128), F32), vrep=((4, 24, 128), F32),
    )
    sems = dict(
        w_sem=(8,), ss=(4,), sr=(4,), os=(10,), orr=(10,), ps=(n,), pr=(n, 3), zs=(n,), zr=(n, 2), cs=(1,), cr=(1,), fs=(3,)
    )
    vmem, hbm, smem = (pl.BlockSpec(memory_space=s) for s in (pltpu.VMEM, pl.ANY, pltpu.SMEM))
    shape = jax.ShapeDtypeStruct
    return pl.pallas_call(
        functools.partial(sum_kernel, INPUTS + SUM_OUT + list(table) + list(sems)),
        out_shape=(
            shape((rows, D), BF), shape((rows, D), F32), shape((UNITS * 16, 2, 2, half, LANES), BF), shape((own, D), F32), shape((24, 128), F32),
        ),
        in_specs=[vmem] * 4 + [smem] + [vmem] * 11 + [hbm] * 8,
        out_specs=(hbm, hbm, hbm, vmem, vmem),
        scratch_shapes=buffers(table) + [pltpu.SemaphoreType.DMA(dims) for dims in sems.values()],
        compiler_params=pltpu.CompilerParams(collective_id=0, has_side_effects=True, vmem_limit_bytes=VMEM_LIMIT),
        cost_estimate=pl.CostEstimate(flops=15 * 10**9, bytes_accessed=5 * 10**7, transcendentals=10**6),
    )(*small_inputs(args), *weight_inputs(args))


def place_kernel(result, d_hidden, fin, dstore, vec, *outs):
    (o_result, o_hidden, o_dstore, o_qkv, o_sbias, o_so, o_sob, o_n1, o_cq, o_cqb, o_ckv, o_cvb, o_co, o_cob, o_n2, o_fi, o_fib, o_fo, o_fob, o_n3) = outs
    o_result[...] = result[...]
    o_hidden[...] = d_hidden[...]
    o_dstore[...] = dstore[...]
    wide = {"qkv": o_qkv, "so": o_so, "cq": o_cq, "ckv": o_ckv, "co": o_co, "fi": o_fi}
    for i, (kind, part) in enumerate(PRODUCTS):
        for c in range(2):
            values = jnp.concatenate([fin[UNITS * i + unit, c] for unit in range(UNITS)], axis=1).astype(F32)
            if kind == "fo":
                begin = c * 2 * SHARD + (part // 2) * SHARD
                o_fo[begin : begin + SHARD, (part % 2) * PART : (part % 2 + 1) * PART] = values
            else:
                ref = wide[kind]
                begin = part * D + c * PART
                ref[:, begin : begin + PART] = values
    for ref, row in ((o_sbias, 0), (o_n1, 3), (o_n2, 8), (o_n3, 11)):
        ref[...] = vec[row : row + 2, 0:SHARD]
    for ref, row in ((o_sob, 2), (o_cqb, 5), (o_cvb, 6), (o_cob, 7), (o_fob, 10)):
        ref[...] = vec[row, 0:SHARD]
    for part in range(4):
        o_fib[pl.ds(part * SHARD, SHARD)] = vec[13 + part, 0:SHARD]


def place(result, d_hidden, fin, dstore, vec):
    shape = lambda *dims: jax.ShapeDtypeStruct(dims, F32)
    return pl.pallas_call(
        place_kernel,
        out_shape=(
            jax.ShapeDtypeStruct(result.shape, BF), shape(*d_hidden.shape), shape(*dstore.shape), shape(SHARD, 3 * D), shape(2, SHARD), shape(SHARD, D), shape(SHARD), shape(2, SHARD),
            shape(SHARD, D), shape(SHARD), shape(SHARD, 2 * D), shape(SHARD), shape(SHARD, D), shape(SHARD), shape(2, SHARD),
            shape(SHARD, FF), shape(FF // 8), shape(FF // 8, D), shape(SHARD), shape(2, SHARD),
        ),
        compiler_params=pltpu.CompilerParams(vmem_limit_bytes=VMEM_LIMIT),
    )(result, d_hidden, fin.reshape(UNITS * len(PRODUCTS), 2, SHARD, LANES), dstore, vec)


def sum_plainly(states, xt, act_t, dmat, dkv, dstore, vec):
    def total(value, dim):
        part = lax.psum_scatter(value, "blk", scatter_dimension=dim, tiled=True)
        return lax.psum(part.astype(BF), "rep").astype(F32)

    at_col = columns(False)

    def rows_of(start):
        return lax.slice_in_dim(xt, start, start + D, axis=0)

    def cols_of(start, width):
        return lax.slice_in_dim(dmat, start, start + width, axis=1)

    g_qkv = total(dot(rows_of(R_TOK), cols_of(at_col.proj, 3 * D)), 0)
    g_so = total(dot(rows_of(R_SMIX), cols_of(at_col.sb, D)), 0)
    g_cq = total(dot(rows_of(R_FIRST), cols_of(at_col.cq, D)), 0)
    g_co = total(dot(rows_of(R_CMIX), cols_of(at_col.cb, D)), 0)
    g_fi = total(dot(rows_of(R_SECOND), cols_of(at_col.inner, FF)), 0)
    g_fo = total(dot(act_t.reshape(FF, -1), cols_of(at_col.fb, D)), 0)
    g_ckv = total(dot_tn(states, dkv), 0)
    g_store = lax.psum_scatter(dstore.astype(F32), "blk", scatter_dimension=0, tiled=True)
    g_fib = total(vec[13:N_VEC].reshape(FF), 0)
    v = total(vec[:13].T, 0)
    two = lambda row: v[:, row : row + 2].T
    return (
        g_store, g_qkv, two(0), g_so, v[:, 2], two(3), g_cq, v[:, 5], g_ckv, v[:, 6], g_co, v[:, 7], two(8),
        g_fi, g_fib, g_fo, v[:, 10], two(11),
    )


def on_device(fast, *args):
    if fast:
        result, d_hidden, *grads = place(*run_sum(args))
    else:
        states_all = lax.all_gather(args[1][0], "blk", axis=0, tiled=True)
        result, d_hidden, *operands = run_plain(args, states_all)
        grads = sum_plainly(states_all, *operands)
    return (result[None, None], d_hidden[None, None], grads[0][None], *grads[1:])


def solution(mesh):
    fast = mesh.shape["blk"] == 8 and mesh.shape["rep"] == 4
    deep, flat = P("rep", "blk", None, None), P("rep", "blk", None)
    in_specs = (deep, flat, deep, deep, P("rep", "blk")) + (P(),) * 17 + (deep,)
    w, vec, two = P("blk", None), P("blk"), P(None, "blk")
    out_specs = (deep, deep, flat, w, two, w, vec, two, w, vec, w, vec, w, vec, two, w, vec, w, vec, two)
    return jax.shard_map(
        functools.partial(on_device, fast), mesh=mesh, in_specs=in_specs, out_specs=out_specs, check_vma=False
    )
```
